128 devices in a mesh: dp: 4 (over z), vocab: 32 (over x, y, core).
Axes of the slice: x: 4, y: 4, z: 4, core: 2. Of those that a mesh axis runs over, the one named last changes fastest.
Arguments:
- input_grad: bfloat16 [65536, 4608], P(('dp', 'vocab')), may hold values from -6 to 6
- token_slab: int32 [65536, 1], P('dp'), may hold values from 0 to 31; in each aligned block of 512 rows (0 to 511, 512 to 1023, ...) at most 32 rows name the same one
- token_offset: int32 [65536, 1], P('dp'), may hold values from 0 to 383
- head_grad: bfloat16 [4, 12288, 4608], P('dp', 'vocab'), may hold values from -6 to 6
- master: float32 [12288, 4608], P(('vocab', 'dp')), may hold values from -0.15625 to 0.15625
- moment_one: float32 [12288, 4608], P(('vocab', 'dp')), may hold values from -4 to 4
- moment_two: float32 [12288, 4608], P(('vocab', 'dp')), may hold values from 0.01 to 1
Outputs:
- master_out: float32 [12288, 4608], P(('vocab', 'dp'))
- moment_one_out: float32 [12288, 4608], P(('vocab', 'dp'))
- moment_two_out: float32 [12288, 4608], P(('vocab', 'dp'))
- table_out: bfloat16 [12288, 4608], P('vocab')
The draws below stay inside these ranges and needn't reach their ends.
Inputs may be any that keep to these rules, and one draw needn't show every extreme that they name: `token_slab`: in each aligned block of 512 rows (one sequence owner's tokens), no slab is named by more than 32 rows.
All inputs are finite; a program needn't handle non-finite values.
Results may differ from the reference program's by a relative error of at most 0.011.
Values may be sent and summed in bfloat16 or wider, within the bound.
No kernel may reach another device: no remote copies, remote signals or barrier semaphores. Data moves between devices by JAX's collectives and lax.ppermute only.
A program may use at most 128 MiB of HBM per device.

```python
import math
import jax
import jax.numpy as jnp
import numpy as np
from jax import lax

D = 4608
TOK_DEV = 512
ROWS_DP = 96
VOCAB = 12288
TOKENS = 65536
CAP = 32
N_DP = 4
N_VOCAB = 32


def with_ends(result, own_key, least, largest):
    dims = result.shape
    spot = [jax.random.randint(jax.random.fold_in(own_key, axis), (), 0, dims[axis]) for axis in range(len(dims))]
    result = result.at[tuple(spot)].set(least)
    longest = dims.index(max(dims))
    spot[longest] = (spot[longest] + 1) % dims[longest]
    return result.at[tuple(spot)].set(largest)


def strengthened(entries, stream_key, source, target, blocks, factor):
    def block_of(position):
        return (jnp.arange(entries.shape[position]) // (entries.shape[position] // blocks)).reshape((-1,) + (1,) * (entries.ndim - 1 - position))

    near = jax.random.permutation(stream_key, blocks)[block_of(target)]
    other_side = (block_of(target) + blocks // 2) % blocks
    return jnp.where((block_of(source) == near) | (block_of(source) == other_side), factor * entries, entries)


def shard_levels(rng, extent, split, least, high):
    level, own = 1.0, jax.random.fold_in(rng, 6)
    for axis_at, parts in split:
        draws = jnp.exp(jax.random.uniform(jax.random.fold_in(own, axis_at), (parts,), jnp.float32, least / len(split), high / len(split)))
        level = level * jnp.repeat(draws, extent[axis_at] // parts).reshape([-1 if axis == axis_at else 1 for axis in range(len(extent))])
    return level


def cumulative_ranks(count, lean):
    portions = [(1 << 20) // math.isqrt(standing ** lean) + 1 for standing in range(1, count + 1)]
    spread = 1 + sum(portions) // (1 << 30)
    return np.cumsum(np.array([max(1, weight // spread) for weight in portions]))


def ranked(own_key, extent, amount, lean):
    listing = cumulative_ranks(amount, lean)
    lot = jax.random.randint(jax.random.fold_in(own_key, 1), extent, 0, int(listing[amount - 1]))
    grade = jnp.searchsorted(jnp.asarray(listing, jnp.int32), lot, side="right")
    return jax.random.permutation(jax.random.fold_in(own_key, 2), amount)[grade].astype(jnp.int32)


def deal_out(key, own, number, rows, number_of, top, reach, lean):
    ranking = jax.random.permutation(key, number_of)
    heavy_load, common = portions_of(number_of, rows * top, reach, lean, True), portions_of(number_of, rows * top, reach, lean, False)
    places = jnp.arange(number_of)

    def named(sizes, rotation):
        used = int((sizes > 0).sum())
        fixed = max(1, used // 4)
        shifted = fixed + (places - fixed + rotation * (used - fixed)) % max(1, number_of - fixed)
        return jnp.zeros((number_of,), jnp.int32).at[ranking[jnp.where(places < fixed, places, shifted)]].set(jnp.asarray(sizes, jnp.int32))

    sizes = jnp.where(number % 4 == 0, named(heavy_load, number // 4), named(common, number - number // 4 - 1))
    mixed = jax.random.permutation(jax.random.fold_in(own, 3), number_of)
    donor, sink = mixed[0:number_of // 2 * 2:2], mixed[1:number_of // 2 * 2:2]
    room = jnp.minimum(sizes[donor] - 1, reach - sizes[sink]) // 2
    room = jnp.where((donor == ranking[0]) | (sink == ranking[0]) | (sizes[sink] == 0), 0, jnp.maximum(room, 0))
    shifted = jax.random.randint(jax.random.fold_in(own, 4), (number_of // 2,), 0, 1 << 20) % (room + 1)
    sizes = sizes.at[donor].add(-shifted).at[sink].add(shifted)
    items = jnp.searchsorted(jnp.cumsum(sizes), jnp.arange(rows * top), side="right").astype(jnp.int32)
    listing = items.reshape(top, rows).T
    listing = listing[jax.random.permutation(jax.random.fold_in(own, 1), rows)]
    rotation = jax.random.randint(jax.random.fold_in(own, 2), (rows, 1), 0, top)
    return jnp.take_along_axis(listing, (jnp.arange(top)[None, :] + rotation) % top, axis=1)


def portions_of(count, total, most, slope, full):
    weights = [(1 << 20) // math.isqrt(standing ** slope) + 1 for standing in range(1, count + 1)]
    largest = most if full else min(most, max(-(-total // count), total * weights[0] // sum(weights)))
    least = 1 if total - largest >= count - 1 else 0
    given, rest = [largest] + [least] * (count - 1), total - largest - least * (count - 1)
    while rest > 0:
        movable = [i for i in range(1, count) if given[i] < largest] or [i for i in range(1, count) if given[i] < most]
        pool, budget = sum([weights[i] for i in movable]), rest
        for i in movable:
            addition = min(most - given[i], max(1, budget * weights[i] // pool), rest)
            given[i] = given[i] + addition
            rest = rest - addition
    return np.array(given)


def gaussian(key, extent, scale, limit, shards=(), kind=jnp.bfloat16):
    array = jax.random.normal(key, extent, jnp.float32) * scale
    if len(shards) > 0:
        array = shard_levels(key, extent, shards, -0.22, 0.18) * array
    return jnp.clip(array, min=-limit, max=limit).astype(kind)


def heavy_noise(own_key, extent, spread, most, cuts, heavy, dtype=jnp.bfloat16):
    values = spread * jax.random.normal(own_key, extent, jnp.float32)
    if cuts:
        values = values * shard_levels(own_key, extent, cuts, -0.22, 0.18)
    return jnp.clip(strengthened(values, jax.random.fold_in(own_key, 3), *heavy), -most, most).astype(dtype)


def setup_inputs(seed: int = 0) -> dict:
    key_list = jax.random.split(jax.random.key(seed), 8)
    input_grad = gaussian(key_list[0], (TOKENS, D), 1.0, 6.0, ((0, 128),))
    token_slab_keys = jax.random.split(jax.random.fold_in(key_list[1], 1), TOKENS // TOK_DEV)
    token_slab_turns = jax.random.permutation(jax.random.fold_in(key_list[1], 3), TOKENS // TOK_DEV)
    token_slab = jax.vmap(lambda own, number: deal_out(jax.random.fold_in(key_list[1], 2), own, number, TOK_DEV, N_VOCAB, 1, CAP, 1))(token_slab_keys, token_slab_turns).reshape((TOKENS, 1))
    token_offset = with_ends(ranked(key_list[2], (TOKENS, 1), ROWS_DP * N_DP, 2), jax.random.fold_in(key_list[2], 3), 0, (ROWS_DP * N_DP) - 1).astype(jnp.int32)
    head_grad = heavy_noise(key_list[3], (N_DP, VOCAB, D), 1.0, 6.0, ((0, 4), (1, 32)), (0, 1, 4, 2.0))
    master = gaussian(key_list[4], (VOCAB, D), 0.01, 0.15625, ((0, 128),), jnp.float32)
    moment_one = gaussian(key_list[5], (VOCAB, D), 0.5, 4.0, ((0, 128),), jnp.float32)
    moment_two = jnp.clip(jnp.exp(math.log(1.0) - 4.6051702 * jax.random.uniform(key_list[6], (VOCAB, D), jnp.float32) ** shard_levels(key_list[6], (VOCAB, D), ((0, 128),), -0.2, 0.2)), 0.01, 1.0)
    return {"input_grad": input_grad, "token_slab": token_slab, "token_offset": token_offset, "head_grad": head_grad, "master": master, "moment_one": moment_one, "moment_two": moment_two}


beta_first = 0.9
beta_second = 0.95
learn_rate = 0.01
weight_decay = 0.1
epsilon = 1e-08
correct_first = 1.0 - 0.9 ** 10
correct_second = 1.0 - 0.95 ** 10

def reference(input_grad, token_slab, token_offset, head_grad, master, moment_one, moment_two):
    slab_rows = ROWS_DP * N_DP
    token_id = (token_slab[:, 0] * slab_rows + token_offset[:, 0]).astype(jnp.int32)
    embed_grad = jnp.zeros((VOCAB, D), jnp.float32).at[token_id].add(input_grad.astype(jnp.float32))
    grad = embed_grad + lax.optimization_barrier(jnp.sum(head_grad.astype(jnp.float32), axis=0))
    first = beta_first * moment_one + (1.0 - beta_first) * grad
    second = beta_second * moment_two + (1.0 - beta_second) * grad * grad
    step_dir = first / correct_first / (jnp.sqrt(second / correct_second) + epsilon) + weight_decay * master
    updated = master - learn_rate * step_dir
    return (updated, first, second, updated.astype(jnp.bfloat16))
```

```python
import jax
import jax.numpy as jnp
from jax import lax
from jax.sharding import PartitionSpec as P

beta_first = 0.9
beta_second = 0.95
learn_rate = 0.01
weight_decay = 0.1
epsilon = 1e-08
correct_first = 1.0 - 0.9**10
correct_second = 1.0 - 0.95**10

CHUNKS = 4


def update(grad, master, moment_one, moment_two):
    first = beta_first * moment_one + (1.0 - beta_first) * grad
    second = beta_second * moment_two + (1.0 - beta_second) * grad * grad
    step_dir = (
        first / correct_first / (jnp.sqrt(second / correct_second) + epsilon)
        + weight_decay * master
    )
    return master - learn_rate * step_dir, first, second


def local(input_grad, token_slab, token_offset, head_grad, master, moment_one, moment_two):
    peers = lax.axis_size("vocab")
    groups = lax.axis_size("dp")
    myself = lax.axis_index("vocab")
    tok_rows, width = input_grad.shape
    slab_rows = head_grad.shape[1]
    capacity = 2 * tok_rows // peers
    slots = peers * capacity
    owners = token_slab[:, 0].reshape(peers, tok_rows)
    offsets = token_offset[:, 0].reshape(peers, tok_rows)

    place = jnp.arange(tok_rows, dtype=jnp.int32)
    earlier = (place[:, None] < place[None, :]).astype(jnp.bfloat16)

    own = lax.dynamic_index_in_dim(owners, myself, 0, keepdims=False)
    named = own[None, :] == jnp.arange(peers, dtype=jnp.int32)[:, None]
    before = jnp.dot(named.astype(jnp.bfloat16), earlier, preferred_element_type=jnp.float32)
    own_rank = jnp.sum(jnp.where(named, before, 0.0), axis=0).astype(jnp.int32)
    slot_of = own * capacity + own_rank
    dispatch = (jnp.arange(slots, dtype=jnp.int32)[:, None] == slot_of[None, :]).astype(jnp.bfloat16)

    mine = owners == myself
    rank = jnp.dot(
        mine.astype(jnp.bfloat16), earlier, preferred_element_type=jnp.float32
    ).astype(jnp.int32)
    held = mine[:, None, :] & (
        rank[:, None, :] == jnp.arange(capacity, dtype=jnp.int32)[None, :, None]
    )
    target = jnp.sum(jnp.where(held, offsets[:, None, :] + 1, 0), axis=2).reshape(-1) - 1
    combine = (jnp.arange(slab_rows, dtype=jnp.int32)[:, None] == target[None, :]).astype(
        jnp.bfloat16
    )

    step = width // CHUNKS
    share = slab_rows // groups
    here = lax.axis_index("dp")
    around = [[(z, (z + hop) % groups) for z in range(groups)] for hop in range(groups)]
    spans = [slice(i * step, (i + 1) * step) for i in range(CHUNKS)]
    table = jnp.zeros((slab_rows, width), jnp.bfloat16)
    results = []
    sent, gathered = [], []
    for i, span in enumerate(spans):
        outgoing = jnp.dot(
            dispatch, input_grad[:, span], preferred_element_type=jnp.float32
        ).astype(jnp.bfloat16)
        if i >= 2:
            outgoing, sent[i - 2] = lax.optimization_barrier((outgoing, sent[i - 2]))
        arrived = lax.all_to_all(outgoing, "vocab", split_axis=0, concat_axis=0, tiled=True)
        partial = jnp.dot(combine, arrived, preferred_element_type=jnp.float32)
        partial = (partial + head_grad[0, :, span].astype(jnp.float32)).astype(jnp.bfloat16)
        pieces = [
            lax.dynamic_slice_in_dim(partial, lax.bitwise_and(here + hop, groups - 1) * share, share, 0)
            for hop in range(groups)
        ]
        sent.append(pieces)
    for i, span in enumerate(spans):
        pieces = sent[i]
        grad = pieces[0].astype(jnp.float32)
        for hop in range(1, groups):
            grad = grad + lax.ppermute(pieces[hop], "dp", around[hop]).astype(jnp.float32)
        updated, first, second = update(
            grad, master[:, span], moment_one[:, span], moment_two[:, span]
        )
        rows = updated.astype(jnp.bfloat16)
        results.append((updated, first, second))
        for hop in range(groups):
            block = rows if hop == 0 else lax.ppermute(rows, "dp", around[hop])
            table = lax.dynamic_update_slice(
                table, block, (lax.bitwise_and(here - hop, groups - 1) * share, i * step)
            )
    return tuple(jnp.concatenate(parts, axis=1) for parts in zip(*results)) + (table,)


def solution(mesh):
    placed = (
        P(("dp", "vocab"), None),
        P("dp", None),
        P("dp", None),
        P("dp", "vocab", None),
        P(("vocab", "dp"), None),
        P(("vocab", "dp"), None),
        P(("vocab", "dp"), None),
    )
    return jax.shard_map(
        local,
        mesh=mesh,
        in_specs=placed,
        out_specs=(
            P(("vocab", "dp"), None),
            P(("vocab", "dp"), None),
            P(("vocab", "dp"), None),
            P("vocab", None),
        ),
        check_vma=False,
    )
```

```python
import functools

import jax
import jax.numpy as jnp
from jax import lax
from jax.experimental import pallas as pl
from jax.experimental.pallas import tpu as pltpu
from jax.sharding import PartitionSpec as P

beta_first = 0.9
beta_second = 0.95
learn_rate = 0.01
weight_decay = 0.1
epsilon = 1e-08
correct_first = 1.0 - 0.9**10
correct_second = 1.0 - 0.95**10

UNITS = (11, 10, 8, 7)


def place_body(start, share, width, here_ref, *refs):
    blocks, table_ref, sems = refs[-6:-2], refs[-2], refs[-1]
    copies = []
    for hop, block_ref in enumerate(blocks):
        row = lax.bitwise_and(here_ref[0] - hop, len(blocks) - 1) * share
        copies.append(
            pltpu.make_async_copy(
                block_ref,
                table_ref.at[pl.ds(pl.multiple_of(row, share), share), pl.ds(start, width)],
                sems.at[hop],
            )
        )
    for copy in copies:
        copy.start()
    for copy in copies:
        copy.wait()


def place(table, here, blocks, start, shape):
    share, width = blocks[0].shape
    anywhere = pl.BlockSpec(memory_space=pl.ANY)
    vmem = pl.BlockSpec(memory_space=pltpu.VMEM)
    before = [] if table is None else [table]
    operands = [here.reshape(1)] + before + blocks
    return pl.pallas_call(
        functools.partial(place_body, start, share, width),
        out_shape=jax.ShapeDtypeStruct(shape, jnp.bfloat16),
        in_specs=[pl.BlockSpec(memory_space=pltpu.SMEM)]
        + [anywhere] * len(before)
        + [vmem] * len(blocks),
        out_specs=anywhere,
        scratch_shapes=[pltpu.SemaphoreType.DMA((len(blocks),))],
        input_output_aliases={} if table is None else {1: 0},
        cost_estimate=pl.CostEstimate(
            flops=0, bytes_accessed=4 * len(blocks) * share * width, transcendentals=0
        ),
    )(*operands)


def update(grad, master, moment_one, moment_two):
    first = beta_first * moment_one + (1.0 - beta_first) * grad
    second = beta_second * moment_two + (1.0 - beta_second) * grad * grad
    step_dir = (
        first / correct_first / (jnp.sqrt(second / correct_second) + epsilon)
        + weight_decay * master
    )
    return master - learn_rate * step_dir, first, second


def local(input_grad, token_slab, token_offset, head_grad, master, moment_one, moment_two):
    peers = lax.axis_size("vocab")
    groups = lax.axis_size("dp")
    myself = lax.axis_index("vocab")
    tok_rows, width = input_grad.shape
    slab_rows = head_grad.shape[1]
    capacity = 2 * tok_rows // peers
    slots = peers * capacity
    owners = token_slab[:, 0].reshape(peers, tok_rows)
    offsets = token_offset[:, 0].reshape(peers, tok_rows)

    order = jnp.arange(tok_rows, dtype=jnp.int32)
    earlier = (order[:, None] < order[None, :]).astype(jnp.bfloat16)

    own = lax.dynamic_index_in_dim(owners, myself, 0, keepdims=False)
    named = own[None, :] == jnp.arange(peers, dtype=jnp.int32)[:, None]
    before = jnp.dot(named.astype(jnp.bfloat16), earlier, preferred_element_type=jnp.float32)
    own_rank = jnp.sum(jnp.where(named, before, 0.0), axis=0).astype(jnp.int32)
    slot_of = own * capacity + own_rank
    dispatch = (jnp.arange(slots, dtype=jnp.int32)[:, None] == slot_of[None, :]).astype(jnp.bfloat16)

    mine = owners == myself
    rank = jnp.dot(
        mine.astype(jnp.bfloat16), earlier, preferred_element_type=jnp.float32
    ).astype(jnp.int32)
    held = mine[:, None, :] & (
        rank[:, None, :] == jnp.arange(capacity, dtype=jnp.int32)[None, :, None]
    )
    target = jnp.sum(jnp.where(held, offsets[:, None, :] + 1, 0), axis=2).reshape(-1) - 1
    combine = (jnp.arange(slab_rows, dtype=jnp.int32)[:, None] == target[None, :]).astype(
        jnp.bfloat16
    )

    share = slab_rows // groups
    here = lax.axis_index("dp")
    around = [[(z, (z + hop) % groups) for z in range(groups)] for hop in range(groups)]
    unit = width // sum(UNITS)
    edges = [unit * sum(UNITS[:i]) for i in range(len(UNITS) + 1)]
    spans = [slice(low, high) for low, high in zip(edges, edges[1:])]

    def send(span):
        return jnp.dot(
            dispatch, input_grad[:, span], preferred_element_type=jnp.float32
        ).astype(jnp.bfloat16)

    def pieces_of(arrived, span):
        partial = jnp.dot(combine, arrived, preferred_element_type=jnp.float32)
        partial = (partial + head_grad[0, :, span].astype(jnp.float32)).astype(jnp.bfloat16)
        return [
            lax.dynamic_slice_in_dim(partial, lax.bitwise_and(here + hop, groups - 1) * share, share, 0)
            for hop in range(groups)
        ]

    def gather(block):
        return [block] + [lax.ppermute(block, "dp", around[hop]) for hop in range(1, groups)]

    last = len(spans) - 1
    states, rows, gathered = [], [], []
    for i, span in enumerate(spans):
        outgoing = send(span)
        if i >= 2:
            outgoing, rows[i - 2] = lax.optimization_barrier((outgoing, rows[i - 2]))
        arrived = lax.all_to_all(outgoing, "vocab", split_axis=0, concat_axis=0, tiled=True)
        if i >= 1:
            arrived, rows[i - 1] = lax.optimization_barrier((arrived, rows[i - 1]))
        pieces = pieces_of(arrived, span)
        if i == last:
            pieces, rows[i - 1] = lax.optimization_barrier((pieces, rows[i - 1]))
        if i >= 1:
            gathered.append(gather(rows[i - 1]))
        grad = pieces[0].astype(jnp.float32)
        for hop in range(1, groups):
            grad = grad + lax.ppermute(pieces[hop], "dp", around[hop]).astype(jnp.float32)
        if 1 <= i < last:
            grad, gathered[i - 1] = lax.optimization_barrier((grad, gathered[i - 1]))
        states.append(update(grad, master[:, span], moment_one[:, span], moment_two[:, span]))
        rows.append(states[-1][0].astype(jnp.bfloat16))
    gathered.append(gather(rows[last]))
    table = None
    for blocks, span in zip(gathered, spans):
        table = place(table, here, blocks, span.start, (slab_rows, width))
    return tuple(jnp.concatenate(parts, axis=1) for parts in zip(*states)) + (table,)


def solution(mesh):
    placed = (
        P(("dp", "vocab"), None),
        P("dp", None),
        P("dp", None),
        P("dp", "vocab", None),
        P(("vocab", "dp"), None),
        P(("vocab", "dp"), None),
        P(("vocab", "dp"), None),
    )
    return jax.shard_map(
        local,
        mesh=mesh,
        in_specs=placed,
        out_specs=(
            P(("vocab", "dp"), None),
            P(("vocab", "dp"), None),
            P(("vocab", "dp"), None),
            P("vocab", None),
        ),
        check_vma=False,
    )
```

```python
import functools

import jax
import jax.numpy as jnp
from jax import lax
from jax.experimental import pallas as pl
from jax.experimental.pallas import tpu as pltpu
from jax.sharding import PartitionSpec as P

beta_first = 0.9
beta_second = 0.95
learn_rate = 0.01
weight_decay = 0.1
epsilon = 1e-08
correct_first = 1.0 - 0.9**10
correct_second = 1.0 - 0.95**10

GROUPS = 4
OWNERS = 32
CAPACITY = 32
UNITS = (12, 10, 8, 6)
TILE = 2
MIB = 1024 * 1024


def after(value, *others):
    return lax.optimization_barrier((value, others))[0]


def swap_z(block, flip):
    return lax.ppermute(block, "dp", [(i, i ^ flip) for i in range(GROUPS)])


def whole(memory_space):
    return pl.BlockSpec(memory_space=memory_space)


def cost(flops, moved):
    return pl.CostEstimate(flops=flops, bytes_accessed=moved, transcendentals=0)


def combine_body(here_ref, target_ref, head_ref, part_ref, own_ref, *refs):
    out_refs, table_ref = (own_ref,) + refs[:-1], refs[-1]
    share = own_ref.shape[0]
    slots = target_ref.shape[1]
    starts = [lax.bitwise_xor(here_ref[0], flip) * share for flip in range(GROUPS)]

    @pl.when(pl.program_id(0) == 0)
    def _():
        for flip, start in enumerate(starts):
            row = lax.broadcasted_iota(jnp.int32, (share, slots), 0) + start
            hit = row == target_ref[...]
            table_ref[pl.ds(flip * share, share), :] = jnp.where(hit, 1.0, 0.0).astype(jnp.bfloat16)

    total = jnp.dot(table_ref[...], part_ref[...], preferred_element_type=jnp.float32)
    for flip, (start, out_ref) in enumerate(zip(starts, out_refs)):
        head = head_ref[0, pl.ds(pl.multiple_of(start, share), share), :].astype(jnp.float32)
        block = total[flip * share : (flip + 1) * share, :] + head
        out_ref[...] = block.astype(out_ref.dtype)


def combine(here, target, head_grad, part, start, tile):
    slots = target.shape[1]
    width = part.shape[1]
    slab_rows = head_grad.shape[1]
    share = slab_rows // GROUPS
    return pl.pallas_call(
        combine_body,
        grid=(width // tile,),
        out_shape=[jax.ShapeDtypeStruct((share, width), jnp.float32)]
        + [jax.ShapeDtypeStruct((share, width), jnp.bfloat16)] * (GROUPS - 1),
        in_specs=[
            whole(pltpu.SMEM),
            pl.BlockSpec((1, slots), lambda i: (0, 0)),
            pl.BlockSpec((1, slab_rows, tile), lambda i: (0, 0, start // tile + i)),
            pl.BlockSpec((slots, tile), lambda i: (0, i)),
        ],
        out_specs=[pl.BlockSpec((share, tile), lambda i: (0, i))] * GROUPS,
        scratch_shapes=[pltpu.VMEM((slab_rows, slots), jnp.bfloat16)],
        compiler_params=pltpu.CompilerParams(vmem_limit_bytes=16 * MIB),
        cost_estimate=cost(2 * slab_rows * slots * width, (2 * slots + 5 * slab_rows) * width),
    )(here.reshape(1), target, head_grad, part)


def place_body(first, spots, share, here_ref, *refs):
    blocks, table_ref, sems = refs[first:-2], refs[-2], refs[-1]
    copies = []
    for at, (block, offset, flip, start) in enumerate(spots):
        row = pl.multiple_of(lax.bitwise_xor(here_ref[0], flip) * share, share)
        source = blocks[block]
        copies.append(
            pltpu.make_async_copy(
                source.at[pl.ds(offset, share), :],
                table_ref.at[pl.ds(row, share), pl.ds(start, source.shape[1])],
                sems.at[at],
            )
        )
    for copy in copies:
        copy.start()
    for copy in copies:
        copy.wait()


def place(table, here, blocks, spots, share, shape):
    before = [] if table is None else [table]
    return pl.pallas_call(
        functools.partial(place_body, len(before), spots, share),
        out_shape=jax.ShapeDtypeStruct(shape, jnp.bfloat16),
        in_specs=[whole(pltpu.SMEM)]
        + [whole(pl.ANY)] * len(before)
        + [whole(pltpu.VMEM)] * len(blocks),
        out_specs=whole(pl.ANY),
        scratch_shapes=[pltpu.SemaphoreType.DMA((len(spots),))],
        input_output_aliases={1: 0} if before else {},
        compiler_params=pltpu.CompilerParams(vmem_limit_bytes=8 * MIB),
        cost_estimate=cost(0, 4 * sum(block.size for block in blocks)),
    )(here.reshape(1), *before, *blocks)


def update(grad, master, moment_one, moment_two):
    first = beta_first * moment_one + (1.0 - beta_first) * grad
    second = beta_second * moment_two + (1.0 - beta_second) * grad * grad
    step_dir = (
        first / correct_first / (jnp.sqrt(second / correct_second) + epsilon)
        + weight_decay * master
    )
    return master - learn_rate * step_dir, first, second


def local(input_grad, token_slab, token_offset, head_grad, master, moment_one, moment_two):
    here, myself = lax.axis_index("dp"), lax.axis_index("vocab")
    tok_rows, width = input_grad.shape
    slab_rows = head_grad.shape[1]
    share = slab_rows // GROUPS
    slots = OWNERS * CAPACITY
    owners = token_slab[:, 0].reshape(OWNERS, tok_rows)
    offsets = token_offset[:, 0].reshape(OWNERS, tok_rows)

    order = jnp.arange(tok_rows, dtype=jnp.int32)
    earlier = (order[:, None] < order[None, :]).astype(jnp.bfloat16)

    own = lax.dynamic_index_in_dim(owners, myself, 0, keepdims=False)
    named = own[None, :] == jnp.arange(OWNERS, dtype=jnp.int32)[:, None]
    before = jnp.dot(named.astype(jnp.bfloat16), earlier, preferred_element_type=jnp.float32)
    own_rank = jnp.sum(jnp.where(named, before, 0.0), axis=0).astype(jnp.int32)
    slot_of = own * CAPACITY + own_rank
    slot_ids = jnp.arange(slots, dtype=jnp.int32)[:, None]

    dispatch = (slot_ids == slot_of[None, :]).astype(jnp.bfloat16)

    mine = owners == myself
    rank = jnp.dot(
        mine.astype(jnp.bfloat16), earlier, preferred_element_type=jnp.float32
    ).astype(jnp.int32)
    held = mine[:, None, :] & (
        rank[:, None, :] == jnp.arange(CAPACITY, dtype=jnp.int32)[None, :, None]
    )
    target = jnp.sum(jnp.where(held, offsets[:, None, :] + 1, 0), axis=2) - 1
    target = target.reshape(1, slots)

    unit = width // sum(UNITS)
    edges = [unit * sum(UNITS[:i]) for i in range(len(UNITS) + 1)]
    spans = [slice(low, high) for low, high in zip(edges, edges[1:])]
    states, rows, joined, fars, blocks, spots = [], [], [], [], [], []
    arrived, last = (), len(spans) - 1
    for number, span in enumerate(spans):
        outgoing = jnp.dot(
            dispatch, input_grad[:, span], preferred_element_type=jnp.float32
        ).astype(jnp.bfloat16)
        earlier_work = target if number == 1 else rows[: max(0, number - 1)]
        outgoing = after(outgoing, arrived, earlier_work)
        arrived = lax.all_to_all(outgoing, "vocab", split_axis=0, concat_axis=0, tiled=True)
        ready = after(arrived, rows)
        grad, *pieces = combine(here, target, head_grad, ready, span.start, TILE * unit)
        if number == last:
            pieces = after(pieces, fars[: number - 1])
        for flip, piece in enumerate(pieces, 1):
            grad = grad + swap_z(piece, flip).astype(jnp.float32)
        if 1 <= number < last:
            grad = after(grad, joined, fars[: number - 1])
        states.append(update(grad, master[:, span], moment_one[:, span], moment_two[:, span]))
        block = states[-1][0].astype(jnp.bfloat16)
        rows.append(block)
        if number < last:
            both = jnp.concatenate([block, swap_z(block, 3)], axis=0)
            joined.append(both)
            spots += [
                (len(blocks), 0, 0, span.start),
                (len(blocks), share, 3, span.start),
                (len(blocks) + 1, 0, 1, span.start),
                (len(blocks) + 1, share, 2, span.start),
            ]
            fars.append(swap_z(both, 1))
            blocks += [both, fars[-1]]
    shape = (slab_rows, width)
    blocks = after(blocks, rows)
    table = place(None, here, blocks, tuple(spots), share, shape)
    blocks = [block] + [swap_z(block, flip) for flip in range(1, GROUPS)]
    spots = [(flip, 0, flip, span.start) for flip in range(GROUPS)]
    table = place(table, here, blocks, tuple(spots), share, shape)
    return tuple(jnp.concatenate(parts, axis=1) for parts in zip(*states)) + (table,)


def solution(mesh):
    placed = (
        P(("dp", "vocab"), None),
        P("dp", None),
        P("dp", None),
        P("dp", "vocab", None),
        P(("vocab", "dp"), None),
        P(("vocab", "dp"), None),
        P(("vocab", "dp"), None),
    )
    return jax.shard_map(
        local,
        mesh=mesh,
        in_specs=placed,
        out_specs=(
            P(("vocab", "dp"), None),
            P(("vocab", "dp"), None),
            P(("vocab", "dp"), None),
            P("vocab", None),
        ),
        check_vma=False,
    )
```

```python
import functools

import jax
import jax.numpy as jnp
from jax import lax
from jax.experimental import pallas as pl
from jax.experimental.pallas import tpu as pltpu
from jax.sharding import PartitionSpec as P

beta_first = 0.9
beta_second = 0.95
learn_rate = 0.01
weight_decay = 0.1
epsilon = 1e-08
correct_first = 1.0 - 0.9**10
correct_second = 1.0 - 0.95**10

GROUPS = 4
OWNERS = 32
CAPACITY = 32
UNITS = (10, 10, 8, 8)
TILE = 2
MIB = 1024 * 1024


def after(value, *others):
    return lax.optimization_barrier((value, others))[0]


def swap_z(block, flip):
    return lax.ppermute(block, "dp", [(i, i ^ flip) for i in range(GROUPS)])


def whole(memory_space):
    return pl.BlockSpec(memory_space=memory_space)


def cost(flops, moved):
    return pl.CostEstimate(flops=flops, bytes_accessed=moved, transcendentals=0)


def combine_body(here_ref, target_ref, head_ref, part_ref, own_ref, *refs):
    out_refs, table_ref = (own_ref,) + refs[:-1], refs[-1]
    share = own_ref.shape[0]
    slots = target_ref.shape[1]
    starts = [lax.bitwise_xor(here_ref[0], flip) * share for flip in range(GROUPS)]

    @pl.when(pl.program_id(0) == 0)
    def _():
        for flip, start in enumerate(starts):
            row = lax.broadcasted_iota(jnp.int32, (share, slots), 0) + start
            hit = row == target_ref[...]
            table_ref[pl.ds(flip * share, share), :] = jnp.where(hit, 1.0, 0.0).astype(jnp.bfloat16)

    total = jnp.dot(table_ref[...], part_ref[...], preferred_element_type=jnp.float32)
    for flip, (start, out_ref) in enumerate(zip(starts, out_refs)):
        head = head_ref[0, pl.ds(pl.multiple_of(start, share), share), :].astype(jnp.float32)
        block = total[flip * share : (flip + 1) * share, :] + head
        out_ref[...] = block.astype(out_ref.dtype)


def combine(here, target, head_grad, part, start, tile):
    slots = target.shape[1]
    width = part.shape[1]
    slab_rows = head_grad.shape[1]
    share = slab_rows // GROUPS
    return pl.pallas_call(
        combine_body,
        grid=(width // tile,),
        out_shape=[jax.ShapeDtypeStruct((share, width), jnp.float32)]
        + [jax.ShapeDtypeStruct((share, width), jnp.bfloat16)] * (GROUPS - 1),
        in_specs=[
            whole(pltpu.SMEM),
            pl.BlockSpec((1, slots), lambda i: (0, 0)),
            pl.BlockSpec((1, slab_rows, tile), lambda i: (0, 0, start // tile + i)),
            pl.BlockSpec((slots, tile), lambda i: (0, i)),
        ],
        out_specs=[pl.BlockSpec((share, tile), lambda i: (0, i))] * GROUPS,
        scratch_shapes=[pltpu.VMEM((slab_rows, slots), jnp.bfloat16)],
        compiler_params=pltpu.CompilerParams(vmem_limit_bytes=16 * MIB),
        cost_estimate=cost(2 * slab_rows * slots * width, (2 * slots + 5 * slab_rows) * width),
    )(here.reshape(1), target, head_grad, part)


def place_body(first, spots, share, here_ref, *refs):
    blocks, table_ref, sems = refs[first:-2], refs[-2], refs[-1]
    copies = []
    for at, (block, offset, flip, start) in enumerate(spots):
        row = pl.multiple_of(lax.bitwise_xor(here_ref[0], flip) * share, share)
        source = blocks[block]
        copies.append(
            pltpu.make_async_copy(
                source.at[pl.ds(offset, share), :],
                table_ref.at[pl.ds(row, share), pl.ds(start, source.shape[1])],
                sems.at[at],
            )
        )
    for copy in copies:
        copy.start()
    for copy in copies:
        copy.wait()


def place(table, here, blocks, spots, share, shape):
    before = [] if table is None else [table]
    return pl.pallas_call(
        functools.partial(place_body, len(before), spots, share),
        out_shape=jax.ShapeDtypeStruct(shape, jnp.bfloat16),
        in_specs=[whole(pltpu.SMEM)]
        + [whole(pl.ANY)] * len(before)
        + [whole(pltpu.VMEM)] * len(blocks),
        out_specs=whole(pl.ANY),
        scratch_shapes=[pltpu.SemaphoreType.DMA((len(spots),))],
        input_output_aliases={1: 0} if before else {},
        compiler_params=pltpu.CompilerParams(vmem_limit_bytes=8 * MIB),
        cost_estimate=cost(0, 4 * sum(block.size for block in blocks)),
    )(here.reshape(1), *before, *blocks)


def update(grad, master, moment_one, moment_two):
    first = beta_first * moment_one + (1.0 - beta_first) * grad
    second = beta_second * moment_two + (1.0 - beta_second) * grad * grad
    step_dir = (
        first / correct_first / (jnp.sqrt(second / correct_second) + epsilon)
        + weight_decay * master
    )
    return master - learn_rate * step_dir, first, second


def local(input_grad, token_slab, token_offset, head_grad, master, moment_one, moment_two):
    here, myself = lax.axis_index("dp"), lax.axis_index("vocab")
    tok_rows, width = input_grad.shape
    slab_rows = head_grad.shape[1]
    share = slab_rows // GROUPS
    slots = OWNERS * CAPACITY
    owners = token_slab[:, 0].reshape(OWNERS, tok_rows)
    offsets = token_offset[:, 0].reshape(OWNERS, tok_rows)

    order = jnp.arange(tok_rows, dtype=jnp.int32)
    earlier = (order[:, None] < order[None, :]).astype(jnp.bfloat16)

    own = lax.dynamic_index_in_dim(owners, myself, 0, keepdims=False)
    named = own[None, :] == jnp.arange(OWNERS, dtype=jnp.int32)[:, None]
    before = jnp.dot(named.astype(jnp.bfloat16), earlier, preferred_element_type=jnp.float32)
    own_rank = jnp.sum(jnp.where(named, before, 0.0), axis=0).astype(jnp.int32)
    slot_of = own * CAPACITY + own_rank
    slot_ids = jnp.arange(slots, dtype=jnp.int32)[:, None]

    dispatch = (slot_ids == slot_of[None, :]).astype(jnp.bfloat16)

    mine = owners == myself
    rank = jnp.dot(
        mine.astype(jnp.bfloat16), earlier, preferred_element_type=jnp.float32
    ).astype(jnp.int32)
    held = mine[:, None, :] & (
        rank[:, None, :] == jnp.arange(CAPACITY, dtype=jnp.int32)[None, :, None]
    )
    target = jnp.sum(jnp.where(held, offsets[:, None, :] + 1, 0), axis=2) - 1
    target = target.reshape(1, slots)

    unit = width // sum(UNITS)
    edges = [unit * sum(UNITS[:i]) for i in range(len(UNITS) + 1)]
    spans = [slice(low, high) for low, high in zip(edges, edges[1:])]
    states, rows, joined, fars, blocks, spots = [], [], [], [], [], []
    arrived, last = (), len(spans) - 1
    for number, span in enumerate(spans):
        outgoing = jnp.dot(
            dispatch, input_grad[:, span], preferred_element_type=jnp.float32
        ).astype(jnp.bfloat16)
        earlier_work = target if number == 1 else rows[: max(0, number - 1)]
        outgoing = after(outgoing, arrived, earlier_work, joined[: max(0, number - 1)])
        arrived = lax.all_to_all(outgoing, "vocab", split_axis=0, concat_axis=0, tiled=True)
        ready = after(arrived, rows)
        grad, *pieces = combine(here, target, head_grad, ready, span.start, TILE * unit)
        for flip, piece in enumerate(pieces, 1):
            grad = grad + swap_z(piece, flip).astype(jnp.float32)
        if 1 <= number < last:
            grad = after(grad, fars)
        states.append(update(grad, master[:, span], moment_one[:, span], moment_two[:, span]))
        block = states[-1][0].astype(jnp.bfloat16)
        rows.append(block)
        if number < last:
            both = jnp.concatenate([block, swap_z(block, 3)], axis=0)
            joined.append(both)
            spots += [
                (len(blocks), 0, 0, span.start),
                (len(blocks), share, 3, span.start),
                (len(blocks) + 1, 0, 1, span.start),
                (len(blocks) + 1, share, 2, span.start),
            ]
            fars.append(swap_z(both, 1))
            blocks += [both, fars[-1]]
    shape = (slab_rows, width)
    blocks = after(blocks, rows)
    table = place(None, here, blocks, tuple(spots), share, shape)
    blocks = [block] + [swap_z(block, flip) for flip in range(1, GROUPS)]
    spots = [(flip, 0, flip, span.start) for flip in range(GROUPS)]
    table = place(table, here, blocks, tuple(spots), share, shape)
    return tuple(jnp.concatenate(parts, axis=1) for parts in zip(*states)) + (table,)


def solution(mesh):
    placed = (
        P(("dp", "vocab"), None),
        P("dp", None),
        P("dp", None),
        P("dp", "vocab", None),
        P(("vocab", "dp"), None),
        P(("vocab", "dp"), None),
        P(("vocab", "dp"), None),
    )
    return jax.shard_map(
        local,
        mesh=mesh,
        in_specs=placed,
        out_specs=(
            P(("vocab", "dp"), None),
            P(("vocab", "dp"), None),
            P(("vocab", "dp"), None),
            P("vocab", None),
        ),
        check_vma=False,
    )
```

```python
import functools

import jax
import jax.numpy as jnp
from jax import lax
from jax.experimental import pallas as pl
from jax.experimental.pallas import tpu as pltpu
from jax.sharding import PartitionSpec as P

beta_first = 0.9
beta_second = 0.95
learn_rate = 0.01
weight_decay = 0.1
epsilon = 1e-08
correct_first = 1.0 - 0.9**10
correct_second = 1.0 - 0.95**10

GROUPS = 4
OWNERS = 32
CAPACITY = 32
UNITS = (12, 8, 8, 8)
HALVES = ((1, 3), (3, 1))
MIB = 1024 * 1024


def after(value, *others):
    return lax.optimization_barrier((value, others))[0]


def swap_z(block, flip):
    return lax.ppermute(block, "dp", [(i, i ^ flip) for i in range(GROUPS)])


def whole(memory_space):
    return pl.BlockSpec(memory_space=memory_space)


def cost(flops, moved):
    return pl.CostEstimate(flops=flops, bytes_accessed=moved, transcendentals=0)


def combine_body(here_ref, target_ref, head_ref, part_ref, *refs):
    table_ref = refs[-1]
    share = head_ref.shape[1] // GROUPS
    slots = target_ref.shape[1]
    starts = [lax.bitwise_xor(here_ref[0], flip) * share for flip in range(GROUPS)]

    @pl.when(pl.program_id(0) == 0)
    def _():
        for flip, start in enumerate(starts):
            row = lax.broadcasted_iota(jnp.int32, (share, slots), 0) + start
            hit = row == target_ref[...]
            table_ref[pl.ds(flip * share, share), :] = jnp.where(hit, 1.0, 0.0).astype(jnp.bfloat16)

    total = jnp.dot(table_ref[...], part_ref[...], preferred_element_type=jnp.float32)
    blocks = []
    for flip, start in enumerate(starts):
        head = head_ref[0, pl.ds(pl.multiple_of(start, share), share), :].astype(jnp.float32)
        blocks.append(total[flip * share : (flip + 1) * share, :] + head)

    for side, (one, two) in enumerate(HALVES):

        @pl.when(pl.program_id(0) == side)
        def _(side=side, one=one, two=two):
            keep_ref, send_ref = refs[2 * side], refs[2 * side + 1]
            for at, flip in enumerate((0, two)):
                keep_ref[pl.ds(at * share, share), :] = blocks[flip]
            for at, flip in enumerate((one, one ^ two)):
                send_ref[pl.ds(at * share, share), :] = blocks[flip].astype(jnp.bfloat16)


def combine(here, target, head_grad, part, start):
    slots = target.shape[1]
    width = part.shape[1]
    slab_rows = head_grad.shape[1]
    tile = width // 2
    kept = jax.ShapeDtypeStruct((slab_rows // 2, tile), jnp.float32)
    sent = jax.ShapeDtypeStruct((slab_rows // 2, tile), jnp.bfloat16)
    return pl.pallas_call(
        combine_body,
        grid=(2,),
        out_shape=[kept, sent] * 2,
        in_specs=[
            whole(pltpu.SMEM),
            pl.BlockSpec((1, slots), lambda i: (0, 0)),
            pl.BlockSpec((1, slab_rows, tile), lambda i: (0, 0, start // tile + i)),
            pl.BlockSpec((slots, tile), lambda i: (0, i)),
        ],
        out_specs=[pl.BlockSpec((slab_rows // 2, tile), lambda i: (0, 0))] * 4,
        scratch_shapes=[pltpu.VMEM((slab_rows, slots), jnp.bfloat16)],
        compiler_params=pltpu.CompilerParams(vmem_limit_bytes=24 * MIB),
        cost_estimate=cost(2 * slab_rows * slots * width, (2 * slots + 5 * slab_rows) * width),
    )(here.reshape(1), target, head_grad, part)


def place_body(first, spots, share, here_ref, *refs):
    blocks, table_ref, sems = refs[first:-2], refs[-2], refs[-1]
    copies = []
    for at, (block, offset, flip, start) in enumerate(spots):
        row = pl.multiple_of(lax.bitwise_xor(here_ref[0], flip) * share, share)
        source = blocks[block]
        copies.append(
            pltpu.make_async_copy(
                source.at[pl.ds(offset, share), :],
                table_ref.at[pl.ds(row, share), pl.ds(start, source.shape[1])],
                sems.at[at],
            )
        )
    for copy in copies:
        copy.start()
    for copy in copies:
        copy.wait()


def place(table, here, blocks, spots, share, shape):
    before = [] if table is None else [table]
    return pl.pallas_call(
        functools.partial(place_body, len(before), spots, share),
        out_shape=jax.ShapeDtypeStruct(shape, jnp.bfloat16),
        in_specs=[whole(pltpu.SMEM)]
        + [whole(pl.ANY)] * len(before)
        + [whole(pltpu.VMEM)] * len(blocks),
        out_specs=whole(pl.ANY),
        scratch_shapes=[pltpu.SemaphoreType.DMA((len(spots),))],
        input_output_aliases={1: 0} if before else {},
        compiler_params=pltpu.CompilerParams(vmem_limit_bytes=8 * MIB),
        cost_estimate=cost(0, 4 * sum(block.size for block in blocks)),
    )(here.reshape(1), *before, *blocks)


def update(grad, master, moment_one, moment_two):
    first = beta_first * moment_one + (1.0 - beta_first) * grad
    second = beta_second * moment_two + (1.0 - beta_second) * grad * grad
    step_dir = (
        first / correct_first / (jnp.sqrt(second / correct_second) + epsilon)
        + weight_decay * master
    )
    return master - learn_rate * step_dir, first, second


def local(input_grad, token_slab, token_offset, head_grad, master, moment_one, moment_two):
    here, myself = lax.axis_index("dp"), lax.axis_index("vocab")
    tok_rows, width = input_grad.shape
    slab_rows = head_grad.shape[1]
    share = slab_rows // GROUPS
    slots = OWNERS * CAPACITY
    owners = token_slab[:, 0].reshape(OWNERS, tok_rows)
    offsets = token_offset[:, 0].reshape(OWNERS, tok_rows)

    order = jnp.arange(tok_rows, dtype=jnp.int32)
    earlier = (order[:, None] < order[None, :]).astype(jnp.bfloat16)

    own = lax.dynamic_index_in_dim(owners, myself, 0, keepdims=False)
    named = own[None, :] == jnp.arange(OWNERS, dtype=jnp.int32)[:, None]
    before = jnp.dot(named.astype(jnp.bfloat16), earlier, preferred_element_type=jnp.float32)
    own_rank = jnp.sum(jnp.where(named, before, 0.0), axis=0).astype(jnp.int32)
    slot_of = own * CAPACITY + own_rank
    slot_ids = jnp.arange(slots, dtype=jnp.int32)[:, None]

    dispatch = (slot_ids == slot_of[None, :]).astype(jnp.bfloat16)

    mine = owners == myself
    rank = jnp.dot(
        mine.astype(jnp.bfloat16), earlier, preferred_element_type=jnp.float32
    ).astype(jnp.int32)
    held = mine[:, None, :] & (
        rank[:, None, :] == jnp.arange(CAPACITY, dtype=jnp.int32)[None, :, None]
    )
    target = jnp.sum(jnp.where(held, offsets[:, None, :] + 1, 0), axis=2) - 1
    target = target.reshape(1, slots)

    unit = width // sum(UNITS)
    edges = [unit * sum(UNITS[:i]) for i in range(len(UNITS) + 1)]
    spans = [slice(low, high) for low, high in zip(edges, edges[1:])]
    states, rows, joined, fars, blocks, spots = [], [], [], [], [], []
    arrived, last = (), len(spans) - 1
    picked = [
        jnp.dot(dispatch, input_grad[:, span], preferred_element_type=jnp.float32).astype(jnp.bfloat16)
        for span in spans
    ]
    for number, span in enumerate(spans):
        outgoing = picked[number]
        earlier_work = target if number == 1 else rows[: max(0, number - 1)]
        outgoing = after(outgoing, arrived, earlier_work)
        arrived = lax.all_to_all(outgoing, "vocab", split_axis=0, concat_axis=0, tiled=True)
        ready = after(arrived, rows, picked[: number + 2])
        sums = combine(here, target, head_grad, ready, span.start)
        grads = []
        for side, (one, two) in enumerate(HALVES):
            keep, sent = sums[2 * side : 2 * side + 2]
            half = swap_z(sent, one).astype(jnp.float32)
            onward = (keep[share:] + half[share:]).astype(jnp.bfloat16)
            if number == last:
                onward = after(onward, fars[: number - 1])
            grads.append(keep[:share] + half[:share] + swap_z(onward, two).astype(jnp.float32))
        grad = jnp.concatenate(grads, axis=1)
        if 1 <= number < last:
            grad = after(grad, fars[: number - 1], joined)
        states.append(update(grad, master[:, span], moment_one[:, span], moment_two[:, span]))
        block = states[-1][0].astype(jnp.bfloat16)
        rows.append(block)
        if number < last:
            both = jnp.concatenate([block, swap_z(block, 3)], axis=0)
            joined.append(both)
            spots += [
                (len(blocks), 0, 0, span.start),
                (len(blocks), share, 3, span.start),
                (len(blocks) + 1, 0, 1, span.start),
                (len(blocks) + 1, share, 2, span.start),
            ]
            fars.append(swap_z(both, 1))
            blocks += [both, fars[-1]]
    shape = (slab_rows, width)
    blocks = after(blocks, rows)
    table = place(None, here, blocks, tuple(spots), share, shape)
    blocks = [block] + [swap_z(block, flip) for flip in range(1, GROUPS)]
    spots = [(flip, 0, flip, span.start) for flip in range(GROUPS)]
    table = place(table, here, blocks, tuple(spots), share, shape)
    return tuple(jnp.concatenate(parts, axis=1) for parts in zip(*states)) + (table,)


def solution(mesh):
    placed = (
        P(("dp", "vocab"), None),
        P("dp", None),
        P("dp", None),
        P("dp", "vocab", None),
        P(("vocab", "dp"), None),
        P(("vocab", "dp"), None),
        P(("vocab", "dp"), None),
    )
    return jax.shard_map(
        local,
        mesh=mesh,
        in_specs=placed,
        out_specs=(
            P(("vocab", "dp"), None),
            P(("vocab", "dp"), None),
            P(("vocab", "dp"), None),
            P("vocab", None),
        ),
        check_vma=False,
    )
```

```python
import functools

import jax
import jax.numpy as jnp
from jax import lax
from jax.experimental import pallas as pl
from jax.experimental.pallas import tpu as pltpu
from jax.sharding import PartitionSpec as P

beta_first = 0.9
beta_second = 0.95
learn_rate = 0.01
weight_decay = 0.1
epsilon = 1e-08
correct_first = 1.0 - 0.9**10
correct_second = 1.0 - 0.95**10

GROUPS = 4
OWNERS = 32
CAPACITY = 32
UNITS = (12, 8, 8, 8)
HALVES = ((1, 3), (3, 1))
MIB = 1024 * 1024


def after(value, *others):
    return lax.optimization_barrier((value, others))[0]


def swap_z(block, flip):
    return lax.ppermute(block, "dp", [(i, i ^ flip) for i in range(GROUPS)])


def whole(memory_space):
    return pl.BlockSpec(memory_space=memory_space)


def cost(flops, moved):
    return pl.CostEstimate(flops=flops, bytes_accessed=moved, transcendentals=0)


def combine_body(here_ref, target_ref, head_ref, part_ref, *refs):
    table_ref = refs[-1]
    share = head_ref.shape[1] // GROUPS
    slots = target_ref.shape[1]
    starts = [lax.bitwise_xor(here_ref[0], flip) * share for flip in range(GROUPS)]

    @pl.when(pl.program_id(0) == 0)
    def _():
        for flip, start in enumerate(starts):
            row = lax.broadcasted_iota(jnp.int32, (share, slots), 0) + start
            hit = row == target_ref[...]
            table_ref[pl.ds(flip * share, share), :] = jnp.where(hit, 1.0, 0.0).astype(jnp.bfloat16)

    total = jnp.dot(table_ref[...], part_ref[...], preferred_element_type=jnp.float32)
    blocks = []
    for flip, start in enumerate(starts):
        head = head_ref[0, pl.ds(pl.multiple_of(start, share), share), :].astype(jnp.float32)
        blocks.append(total[flip * share : (flip + 1) * share, :] + head)

    for side, (one, two) in enumerate(HALVES):

        @pl.when(pl.program_id(0) == side)
        def _(side=side, one=one, two=two):
            keep_ref, send_ref = refs[2 * side], refs[2 * side + 1]
            for at, flip in enumerate((0, two)):
                keep_ref[pl.ds(at * share, share), :] = blocks[flip]
            for at, flip in enumerate((one, one ^ two)):
                send_ref[pl.ds(at * share, share), :] = blocks[flip].astype(jnp.bfloat16)


def combine(here, target, head_grad, part, start):
    slots = target.shape[1]
    width = part.shape[1]
    slab_rows = head_grad.shape[1]
    tile = width // 2
    kept = jax.ShapeDtypeStruct((slab_rows // 2, tile), jnp.float32)
    sent = jax.ShapeDtypeStruct((slab_rows // 2, tile), jnp.bfloat16)
    return pl.pallas_call(
        combine_body,
        grid=(2,),
        out_shape=[kept, sent] * 2,
        in_specs=[
            whole(pltpu.SMEM),
            pl.BlockSpec((1, slots), lambda i: (0, 0)),
            pl.BlockSpec((1, slab_rows, tile), lambda i: (0, 0, start // tile + i)),
            pl.BlockSpec((slots, tile), lambda i: (0, i)),
        ],
        out_specs=[pl.BlockSpec((slab_rows // 2, tile), lambda i: (0, 0))] * 4,
        scratch_shapes=[pltpu.VMEM((slab_rows, slots), jnp.bfloat16)],
        compiler_params=pltpu.CompilerParams(vmem_limit_bytes=24 * MIB),
        cost_estimate=cost(2 * slab_rows * slots * width, (2 * slots + 5 * slab_rows) * width),
    )(here.reshape(1), target, head_grad, part)


def place_body(first, spots, share, here_ref, *refs):
    blocks, table_ref, sems = refs[first:-2], refs[-2], refs[-1]
    copies = []
    for at, (block, offset, flip, start) in enumerate(spots):
        row = pl.multiple_of(lax.bitwise_xor(here_ref[0], flip) * share, share)
        source = blocks[block]
        copies.append(
            pltpu.make_async_copy(
                source.at[pl.ds(offset, share), :],
                table_ref.at[pl.ds(row, share), pl.ds(start, source.shape[1])],
                sems.at[at],
            )
        )
    for copy in copies:
        copy.start()
    for copy in copies:
        copy.wait()


def place(table, here, blocks, spots, share, shape):
    before = [] if table is None else [table]
    return pl.pallas_call(
        functools.partial(place_body, len(before), spots, share),
        out_shape=jax.ShapeDtypeStruct(shape, jnp.bfloat16),
        in_specs=[whole(pltpu.SMEM)]
        + [whole(pl.ANY)] * len(before)
        + [whole(pltpu.VMEM)] * len(blocks),
        out_specs=whole(pl.ANY),
        scratch_shapes=[pltpu.SemaphoreType.DMA((len(spots),))],
        input_output_aliases={1: 0} if before else {},
        compiler_params=pltpu.CompilerParams(vmem_limit_bytes=8 * MIB),
        cost_estimate=cost(0, 4 * sum(block.size for block in blocks)),
    )(here.reshape(1), *before, *blocks)


def update(grad, master, moment_one, moment_two):
    first = beta_first * moment_one + (1.0 - beta_first) * grad
    second = beta_second * moment_two + (1.0 - beta_second) * grad * grad
    step_dir = (
        first / correct_first / (jnp.sqrt(second / correct_second) + epsilon)
        + weight_decay * master
    )
    return master - learn_rate * step_dir, first, second


def local(input_grad, token_slab, token_offset, head_grad, master, moment_one, moment_two):
    here, myself = lax.axis_index("dp"), lax.axis_index("vocab")
    tok_rows, width = input_grad.shape
    slab_rows = head_grad.shape[1]
    share = slab_rows // GROUPS
    slots = OWNERS * CAPACITY
    owners = token_slab[:, 0].reshape(OWNERS, tok_rows)
    offsets = token_offset[:, 0].reshape(OWNERS, tok_rows)

    order = jnp.arange(tok_rows, dtype=jnp.int32)
    earlier = (order[:, None] < order[None, :]).astype(jnp.bfloat16)

    own = lax.dynamic_index_in_dim(owners, myself, 0, keepdims=False)
    named = own[None, :] == jnp.arange(OWNERS, dtype=jnp.int32)[:, None]
    before = jnp.dot(named.astype(jnp.bfloat16), earlier, preferred_element_type=jnp.float32)
    own_rank = jnp.sum(jnp.where(named, before, 0.0), axis=0).astype(jnp.int32)
    slot_of = own * CAPACITY + own_rank
    slot_ids = jnp.arange(slots, dtype=jnp.int32)[:, None]

    dispatch = (slot_ids == slot_of[None, :]).astype(jnp.bfloat16)

    mine = owners == myself
    rank = jnp.dot(
        mine.astype(jnp.bfloat16), earlier, preferred_element_type=jnp.float32
    ).astype(jnp.int32)
    held = mine[:, None, :] & (
        rank[:, None, :] == jnp.arange(CAPACITY, dtype=jnp.int32)[None, :, None]
    )
    target = jnp.sum(jnp.where(held, offsets[:, None, :] + 1, 0), axis=2) - 1
    target = target.reshape(1, slots)

    unit = width // sum(UNITS)
    edges = [unit * sum(UNITS[:i]) for i in range(len(UNITS) + 1)]
    spans = [slice(low, high) for low, high in zip(edges, edges[1:])]
    states, rows, blocks, spots = [], [], [], []
    arrived, last = (), len(spans) - 1
    picked = [
        jnp.dot(dispatch, input_grad[:, span], preferred_element_type=jnp.float32).astype(jnp.bfloat16)
        for span in spans
    ]
    for number, span in enumerate(spans):
        outgoing = picked[number]
        earlier_work = (target, picked) if number == 1 else rows[: max(0, number - 1)]
        outgoing = after(outgoing, arrived, earlier_work)
        arrived = lax.all_to_all(outgoing, "vocab", split_axis=0, concat_axis=0, tiled=True)
        ready = after(arrived, rows, blocks if number == last else ())
        sums = combine(here, target, head_grad, ready, span.start)
        grads, onwards = [], []
        for side, (one, two) in enumerate(HALVES):
            keep, sent = sums[2 * side : 2 * side + 2]
            half = swap_z(sent, one).astype(jnp.float32)
            onwards.append((keep[share:] + half[share:]).astype(jnp.bfloat16))
            came = swap_z(onwards[side], two).astype(jnp.float32)
            grads.append(keep[:share] + half[:share] + came)
        grad = jnp.concatenate(grads, axis=1)
        if number:
            one, two = HALVES[number % 2]
            near = swap_z(rows[-1], one)
            if number > 1:
                near = after(near, onwards)
            both = jnp.concatenate([rows[-1], near], axis=0)
            far = swap_z(both, two)
            start = spans[number - 1].start
            spots += [
                (len(blocks), 0, 0, start),
                (len(blocks), share, one, start),
                (len(blocks) + 1, 0, two, start),
                (len(blocks) + 1, share, one ^ two, start),
            ]
            blocks += [both, far]
            if number < last:
                grad = after(grad, far if number == 1 else both)
        states.append(update(grad, master[:, span], moment_one[:, span], moment_two[:, span]))
        rows.append(states[-1][0].astype(jnp.bfloat16))
    shape = (slab_rows, width)
    blocks = after(blocks, rows)
    table = place(None, here, blocks, tuple(spots), share, shape)
    blocks = [rows[last]] + [swap_z(rows[last], flip) for flip in range(1, GROUPS)]
    spots = [(flip, 0, flip, span.start) for flip in range(GROUPS)]
    table = place(table, here, blocks, tuple(spots), share, shape)
    return tuple(jnp.concatenate(parts, axis=1) for parts in zip(*states)) + (table,)


def solution(mesh):
    placed = (
        P(("dp", "vocab"), None),
        P("dp", None),
        P("dp", None),
        P("dp", "vocab", None),
        P(("vocab", "dp"), None),
        P(("vocab", "dp"), None),
        P(("vocab", "dp"), None),
    )
    return jax.shard_map(
        local,
        mesh=mesh,
        in_specs=placed,
        out_specs=(
            P(("vocab", "dp"), None),
            P(("vocab", "dp"), None),
            P(("vocab", "dp"), None),
            P("vocab", None),
        ),
        check_vma=False,
    )
```

```python
import functools

import jax
import jax.numpy as jnp
from jax import lax
from jax.experimental import pallas as pl
from jax.experimental.pallas import tpu as pltpu
from jax.sharding import PartitionSpec as P

beta_first = 0.9
beta_second = 0.95
learn_rate = 0.01
weight_decay = 0.1
epsilon = 1e-08
correct_first = 1.0 - 0.9**10
correct_second = 1.0 - 0.95**10

GROUPS = 4
OWNERS = 32
CAPACITY = 32
UNITS = (10, 10, 10, 6)
HALVES = ((1, 3), (3, 1))
MIB = 1024 * 1024


def after(value, *others):
    return lax.optimization_barrier((value, others))[0]


def swap_z(block, flip):
    return lax.ppermute(block, "dp", [(i, i ^ flip) for i in range(GROUPS)])


def whole(memory_space):
    return pl.BlockSpec(memory_space=memory_space)


def cost(flops, moved):
    return pl.CostEstimate(flops=flops, bytes_accessed=moved, transcendentals=0)


def combine_body(here_ref, target_ref, head_ref, part_ref, *refs):
    table_ref = refs[-1]
    share = head_ref.shape[1] // GROUPS
    slots = target_ref.shape[1]
    starts = [lax.bitwise_xor(here_ref[0], flip) * share for flip in range(GROUPS)]

    @pl.when(pl.program_id(0) == 0)
    def _():
        for flip, start in enumerate(starts):
            row = lax.broadcasted_iota(jnp.int32, (share, slots), 0) + start
            hit = row == target_ref[...]
            table_ref[pl.ds(flip * share, share), :] = jnp.where(hit, 1.0, 0.0).astype(jnp.bfloat16)

    total = jnp.dot(table_ref[...], part_ref[...], preferred_element_type=jnp.float32)
    blocks = []
    for flip, start in enumerate(starts):
        head = head_ref[0, pl.ds(pl.multiple_of(start, share), share), :].astype(jnp.float32)
        blocks.append(total[flip * share : (flip + 1) * share, :] + head)

    for side, (one, two) in enumerate(HALVES):

        @pl.when(pl.program_id(0) == side)
        def _(side=side, one=one, two=two):
            keep_ref, send_ref = refs[2 * side], refs[2 * side + 1]
            for at, flip in enumerate((0, two)):
                keep_ref[pl.ds(at * share, share), :] = blocks[flip]
            for at, flip in enumerate((one, one ^ two)):
                send_ref[pl.ds(at * share, share), :] = blocks[flip].astype(jnp.bfloat16)


def combine(here, target, head_grad, part, start):
    slots = target.shape[1]
    width = part.shape[1]
    slab_rows = head_grad.shape[1]
    tile = width // 2
    kept = jax.ShapeDtypeStruct((slab_rows // 2, tile), jnp.float32)
    sent = jax.ShapeDtypeStruct((slab_rows // 2, tile), jnp.bfloat16)
    return pl.pallas_call(
        combine_body,
        grid=(2,),
        out_shape=[kept, sent] * 2,
        in_specs=[
            whole(pltpu.SMEM),
            pl.BlockSpec((1, slots), lambda i: (0, 0)),
            pl.BlockSpec((1, slab_rows, tile), lambda i: (0, 0, start // tile + i)),
            pl.BlockSpec((slots, tile), lambda i: (0, i)),
        ],
        out_specs=[pl.BlockSpec((slab_rows // 2, tile), lambda i: (0, 0))] * 4,
        scratch_shapes=[pltpu.VMEM((slab_rows, slots), jnp.bfloat16)],
        compiler_params=pltpu.CompilerParams(vmem_limit_bytes=24 * MIB),
        cost_estimate=cost(2 * slab_rows * slots * width, (2 * slots + 5 * slab_rows) * width),
    )(here.reshape(1), target, head_grad, part)


def place_body(first, spots, share, here_ref, *refs):
    blocks, table_ref, sems = refs[first:-2], refs[-2], refs[-1]
    copies = []
    for at, (block, offset, flip, start) in enumerate(spots):
        row = pl.multiple_of(lax.bitwise_xor(here_ref[0], flip) * share, share)
        source = blocks[block]
        copies.append(
            pltpu.make_async_copy(
                source.at[pl.ds(offset, share), :],
                table_ref.at[pl.ds(row, share), pl.ds(start, source.shape[1])],
                sems.at[at],
            )
        )
    for copy in copies:
        copy.start()
    for copy in copies:
        copy.wait()


def place(table, here, blocks, spots, share, shape):
    before = [] if table is None else [table]
    return pl.pallas_call(
        functools.partial(place_body, len(before), spots, share),
        out_shape=jax.ShapeDtypeStruct(shape, jnp.bfloat16),
        in_specs=[whole(pltpu.SMEM)]
        + [whole(pl.ANY)] * len(before)
        + [whole(pltpu.VMEM)] * len(blocks),
        out_specs=whole(pl.ANY),
        scratch_shapes=[pltpu.SemaphoreType.DMA((len(spots),))],
        input_output_aliases={1: 0} if before else {},
        compiler_params=pltpu.CompilerParams(vmem_limit_bytes=8 * MIB),
        cost_estimate=cost(0, 4 * sum(block.size for block in blocks)),
    )(here.reshape(1), *before, *blocks)


def update(grad, master, moment_one, moment_two):
    first = beta_first * moment_one + (1.0 - beta_first) * grad
    second = beta_second * moment_two + (1.0 - beta_second) * grad * grad
    step_dir = (
        first / correct_first / (jnp.sqrt(second / correct_second) + epsilon)
        + weight_decay * master
    )
    return master - learn_rate * step_dir, first, second


def local(input_grad, token_slab, token_offset, head_grad, master, moment_one, moment_two):
    here, myself = lax.axis_index("dp"), lax.axis_index("vocab")
    tok_rows, width = input_grad.shape
    slab_rows = head_grad.shape[1]
    share = slab_rows // GROUPS
    slots = OWNERS * CAPACITY
    owners = token_slab[:, 0].reshape(OWNERS, tok_rows)
    offsets = token_offset[:, 0].reshape(OWNERS, tok_rows)

    order = jnp.arange(tok_rows, dtype=jnp.int32)
    earlier = (order[:, None] < order[None, :]).astype(jnp.bfloat16)

    own = lax.dynamic_index_in_dim(owners, myself, 0, keepdims=False)
    named = own[None, :] == jnp.arange(OWNERS, dtype=jnp.int32)[:, None]
    before = jnp.dot(named.astype(jnp.bfloat16), earlier, preferred_element_type=jnp.float32)
    own_rank = jnp.sum(jnp.where(named, before, 0.0), axis=0).astype(jnp.int32)
    slot_of = own * CAPACITY + own_rank
    slot_ids = jnp.arange(slots, dtype=jnp.int32)[:, None]

    dispatch = (slot_ids == slot_of[None, :]).astype(jnp.bfloat16)

    mine = owners == myself
    rank = jnp.dot(
        mine.astype(jnp.bfloat16), earlier, preferred_element_type=jnp.float32
    ).astype(jnp.int32)
    held = mine[:, None, :] & (
        rank[:, None, :] == jnp.arange(CAPACITY, dtype=jnp.int32)[None, :, None]
    )
    target = jnp.sum(jnp.where(held, offsets[:, None, :] + 1, 0), axis=2) - 1
    target = target.reshape(1, slots)

    unit = width // sum(UNITS)
    edges = [unit * sum(UNITS[:i]) for i in range(len(UNITS) + 1)]
    spans = [slice(low, high) for low, high in zip(edges, edges[1:])]
    states, rows, blocks, spots = [], [], [], []
    arrived, last = (), len(spans) - 1
    picked = [
        jnp.dot(dispatch, input_grad[:, span], preferred_element_type=jnp.float32).astype(jnp.bfloat16)
        for span in spans
    ]
    for number, span in enumerate(spans):
        outgoing = picked[number]
        earlier_work = (target, picked) if number == 1 else rows[: max(0, number - 1)]
        outgoing = after(outgoing, arrived, earlier_work)
        arrived = lax.all_to_all(outgoing, "vocab", split_axis=0, concat_axis=0, tiled=True)
        ready = after(arrived, (rows[:-1], onwards) if number == last else rows)
        sums = combine(here, target, head_grad, ready, span.start)
        grads, onwards = [], []
        for side, (one, two) in enumerate(HALVES):
            keep, sent = sums[2 * side : 2 * side + 2]
            half = swap_z(sent, one).astype(jnp.float32)
            onwards.append((keep[share:] + half[share:]).astype(jnp.bfloat16))
            came = swap_z(onwards[side], two).astype(jnp.float32)
            grads.append(keep[:share] + half[:share] + came)
        grad = jnp.concatenate(grads, axis=1)
        if number:
            one, two = HALVES[number % 2]
            near = swap_z(rows[-1], one)
            if number > 1:
                near = after(near, onwards)
            both = jnp.concatenate([rows[-1], near], axis=0)
            far = swap_z(both, two)
            start = spans[number - 1].start
            spots += [
                (len(blocks), 0, 0, start),
                (len(blocks), share, one, start),
                (len(blocks) + 1, 0, two, start),
                (len(blocks) + 1, share, one ^ two, start),
            ]
            blocks += [both, far]
            if number < last:
                grad = after(grad, far if number == 1 else both)
        states.append(update(grad, master[:, span], moment_one[:, span], moment_two[:, span]))
        rows.append(states[-1][0].astype(jnp.bfloat16))
    shape = (slab_rows, width)
    blocks = after(blocks, rows)
    table = place(None, here, blocks, tuple(spots), share, shape)
    blocks = [rows[last]] + [swap_z(rows[last], flip) for flip in range(1, GROUPS)]
    spots = [(flip, 0, flip, span.start) for flip in range(GROUPS)]
    table = place(table, here, blocks, tuple(spots), share, shape)
    return tuple(jnp.concatenate(parts, axis=1) for parts in zip(*states)) + (table,)


def solution(mesh):
    placed = (
        P(("dp", "vocab"), None),
        P("dp", None),
        P("dp", None),
        P("dp", "vocab", None),
        P(("vocab", "dp"), None),
        P(("vocab", "dp"), None),
        P(("vocab", "dp"), None),
    )
    return jax.shard_map(
        local,
        mesh=mesh,
        in_specs=placed,
        out_specs=(
            P(("vocab", "dp"), None),
            P(("vocab", "dp"), None),
            P(("vocab", "dp"), None),
            P("vocab", None),
        ),
        check_vma=False,
    )
```

```python
import functools

import jax
import jax.numpy as jnp
from jax import lax
from jax.experimental import pallas as pl
from jax.experimental.pallas import tpu as pltpu
from jax.sharding import PartitionSpec as P

beta_first = 0.9
beta_second = 0.95
learn_rate = 0.01
weight_decay = 0.1
epsilon = 1e-08
correct_first = 1.0 - 0.9**10
correct_second = 1.0 - 0.95**10

GROUPS = 4
OWNERS = 32
CAPACITY = 32
UNITS = (8, 10, 10, 8)
TILE = 2
MIB = 1024 * 1024


def after(value, *others):
    return lax.optimization_barrier((value, others))[0]


def swap_z(block, flip):
    return lax.ppermute(block, "dp", [(i, i ^ flip) for i in range(GROUPS)])


def whole(memory_space):
    return pl.BlockSpec(memory_space=memory_space)


def cost(flops, moved):
    return pl.CostEstimate(flops=flops, bytes_accessed=moved, transcendentals=0)


def combine_body(here_ref, target_ref, head_ref, part_ref, own_ref, *refs):
    out_refs, table_ref = (own_ref,) + refs[:-1], refs[-1]
    share = own_ref.shape[0]
    slots = target_ref.shape[1]
    starts = [lax.bitwise_xor(here_ref[0], flip) * share for flip in range(GROUPS)]

    @pl.when(pl.program_id(0) == 0)
    def _():
        for flip, start in enumerate(starts):
            row = lax.broadcasted_iota(jnp.int32, (share, slots), 0) + start
            hit = row == target_ref[...]
            table_ref[pl.ds(flip * share, share), :] = jnp.where(hit, 1.0, 0.0).astype(jnp.bfloat16)

    total = jnp.dot(table_ref[...], part_ref[...], preferred_element_type=jnp.float32)
    for flip, (start, out_ref) in enumerate(zip(starts, out_refs)):
        head = head_ref[0, pl.ds(pl.multiple_of(start, share), share), :].astype(jnp.float32)
        block = total[flip * share : (flip + 1) * share, :] + head
        out_ref[...] = block.astype(out_ref.dtype)


def combine(here, target, head_grad, part, start, tile):
    slots = target.shape[1]
    width = part.shape[1]
    slab_rows = head_grad.shape[1]
    share = slab_rows // GROUPS
    return pl.pallas_call(
        combine_body,
        grid=(width // tile,),
        out_shape=[jax.ShapeDtypeStruct((share, width), jnp.float32)]
        + [jax.ShapeDtypeStruct((share, width), jnp.bfloat16)] * (GROUPS - 1),
        in_specs=[
            whole(pltpu.SMEM),
            pl.BlockSpec((1, slots), lambda i: (0, 0)),
            pl.BlockSpec((1, slab_rows, tile), lambda i: (0, 0, start // tile + i)),
            pl.BlockSpec((slots, tile), lambda i: (0, i)),
        ],
        out_specs=[pl.BlockSpec((share, tile), lambda i: (0, i))] * GROUPS,
        scratch_shapes=[pltpu.VMEM((slab_rows, slots), jnp.bfloat16)],
        compiler_params=pltpu.CompilerParams(vmem_limit_bytes=16 * MIB),
        cost_estimate=cost(2 * slab_rows * slots * width, (2 * slots + 5 * slab_rows) * width),
    )(here.reshape(1), target, head_grad, part)


def place_body(first, spots, share, here_ref, *refs):
    blocks, table_ref, sems = refs[first:-2], refs[-2], refs[-1]
    copies = []
    for at, (block, offset, flip, start) in enumerate(spots):
        row = pl.multiple_of(lax.bitwise_xor(here_ref[0], flip) * share, share)
        source = blocks[block]
        copies.append(
            pltpu.make_async_copy(
                source.at[pl.ds(offset, share), :],
                table_ref.at[pl.ds(row, share), pl.ds(start, source.shape[1])],
                sems.at[at],
            )
        )
    for copy in copies:
        copy.start()
    for copy in copies:
        copy.wait()


def place(table, here, blocks, spots, share, shape):
    before = [] if table is None else [table]
    return pl.pallas_call(
        functools.partial(place_body, len(before), spots, share),
        out_shape=jax.ShapeDtypeStruct(shape, jnp.bfloat16),
        in_specs=[whole(pltpu.SMEM)]
        + [whole(pl.ANY)] * len(before)
        + [whole(pltpu.VMEM)] * len(blocks),
        out_specs=whole(pl.ANY),
        scratch_shapes=[pltpu.SemaphoreType.DMA((len(spots),))],
        input_output_aliases={1: 0} if before else {},
        compiler_params=pltpu.CompilerParams(vmem_limit_bytes=8 * MIB),
        cost_estimate=cost(0, 4 * sum(block.size for block in blocks)),
    )(here.reshape(1), *before, *blocks)


def update(grad, master, moment_one, moment_two):
    first = beta_first * moment_one + (1.0 - beta_first) * grad
    second = beta_second * moment_two + (1.0 - beta_second) * grad * grad
    step_dir = (
        first / correct_first / (jnp.sqrt(second / correct_second) + epsilon)
        + weight_decay * master
    )
    return master - learn_rate * step_dir, first, second


def local(input_grad, token_slab, token_offset, head_grad, master, moment_one, moment_two):
    here, myself = lax.axis_index("dp"), lax.axis_index("vocab")
    tok_rows, width = input_grad.shape
    slab_rows = head_grad.shape[1]
    share = slab_rows // GROUPS
    slots = OWNERS * CAPACITY
    owners = token_slab[:, 0].reshape(OWNERS, tok_rows)
    offsets = token_offset[:, 0].reshape(OWNERS, tok_rows)

    order = jnp.arange(tok_rows, dtype=jnp.int32)
    earlier = (order[:, None] < order[None, :]).astype(jnp.bfloat16)

    own = lax.dynamic_index_in_dim(owners, myself, 0, keepdims=False)
    named = own[None, :] == jnp.arange(OWNERS, dtype=jnp.int32)[:, None]
    before = jnp.dot(named.astype(jnp.bfloat16), earlier, preferred_element_type=jnp.float32)
    own_rank = jnp.sum(jnp.where(named, before, 0.0), axis=0).astype(jnp.int32)
    slot_of = own * CAPACITY + own_rank
    slot_ids = jnp.arange(slots, dtype=jnp.int32)[:, None]

    dispatch = (slot_ids == slot_of[None, :]).astype(jnp.bfloat16)

    mine = owners == myself
    rank = jnp.dot(
        mine.astype(jnp.bfloat16), earlier, preferred_element_type=jnp.float32
    ).astype(jnp.int32)
    held = mine[:, None, :] & (
        rank[:, None, :] == jnp.arange(CAPACITY, dtype=jnp.int32)[None, :, None]
    )
    target = jnp.sum(jnp.where(held, offsets[:, None, :] + 1, 0), axis=2) - 1
    target = target.reshape(1, slots)

    unit = width // sum(UNITS)
    edges = [unit * sum(UNITS[:i]) for i in range(len(UNITS) + 1)]
    spans = [slice(low, high) for low, high in zip(edges, edges[1:])]
    states, rows, joined, fars, blocks, spots = [], [], [], [], [], []
    arrived, last = (), len(spans) - 1
    picked = [
        jnp.dot(dispatch, input_grad[:, span], preferred_element_type=jnp.float32).astype(jnp.bfloat16)
        for span in spans
    ]
    for number, span in enumerate(spans):
        outgoing = picked[number]
        earlier_work = (target, picked) if number == 1 else rows[: max(0, number - 1)]
        outgoing = after(outgoing, arrived, earlier_work, joined[: max(0, number - 1)])
        outgoing = after(outgoing, fars[: max(0, number - 2)])
        arrived = lax.all_to_all(outgoing, "vocab", split_axis=0, concat_axis=0, tiled=True)
        ready = after(arrived, rows)
        grad, *pieces = combine(here, target, head_grad, ready, span.start, TILE * unit)
        if number == last:
            pieces = after(pieces, fars[: number - 1])
        for flip, piece in enumerate(pieces, 1):
            grad = grad + swap_z(piece, flip).astype(jnp.float32)
        states.append(update(grad, master[:, span], moment_one[:, span], moment_two[:, span]))
        block = states[-1][0].astype(jnp.bfloat16)
        rows.append(block)
        if number < last:
            both = jnp.concatenate([block, swap_z(block, 3)], axis=0)
            joined.append(both)
            spots += [
                (len(blocks), 0, 0, span.start),
                (len(blocks), share, 3, span.start),
                (len(blocks) + 1, 0, 1, span.start),
                (len(blocks) + 1, share, 2, span.start),
            ]
            fars.append(swap_z(both, 1))
            blocks += [both, fars[-1]]
    shape = (slab_rows, width)
    blocks = after(blocks, rows)
    table = place(None, here, blocks, tuple(spots), share, shape)
    blocks = [block] + [swap_z(block, flip) for flip in range(1, GROUPS)]
    spots = [(flip, 0, flip, span.start) for flip in range(GROUPS)]
    table = place(table, here, blocks, tuple(spots), share, shape)
    return tuple(jnp.concatenate(parts, axis=1) for parts in zip(*states)) + (table,)


def solution(mesh):
    placed = (
        P(("dp", "vocab"), None),
        P("dp", None),
        P("dp", None),
        P("dp", "vocab", None),
        P(("vocab", "dp"), None),
        P(("vocab", "dp"), None),
        P(("vocab", "dp"), None),
    )
    return jax.shard_map(
        local,
        mesh=mesh,
        in_specs=placed,
        out_specs=(
            P(("vocab", "dp"), None),
            P(("vocab", "dp"), None),
            P(("vocab", "dp"), None),
            P("vocab", None),
        ),
        check_vma=False,
    )
```

```python
import functools

import jax
import jax.numpy as jnp
from jax import lax
from jax.experimental import pallas as pl
from jax.experimental.pallas import tpu as pltpu
from jax.sharding import PartitionSpec as P

beta_first = 0.9
beta_second = 0.95
learn_rate = 0.01
weight_decay = 0.1
epsilon = 1e-08
correct_first = 1.0 - 0.9**10
correct_second = 1.0 - 0.95**10

GROUPS = 4
OWNERS = 32
CAPACITY = 32
UNITS = (8, 10, 10, 8)
TILE = 2
MIB = 1024 * 1024


def after(value, *others):
    return lax.optimization_barrier((value, others))[0]


def swap_z(block, flip):
    return lax.ppermute(block, "dp", [(i, i ^ flip) for i in range(GROUPS)])


def whole(memory_space):
    return pl.BlockSpec(memory_space=memory_space)


def cost(flops, moved):
    return pl.CostEstimate(flops=flops, bytes_accessed=moved, transcendentals=0)


def combine_body(here_ref, target_ref, head_ref, part_ref, own_ref, *refs):
    out_refs, table_ref = (own_ref,) + refs[:-1], refs[-1]
    share = own_ref.shape[0]
    slots = target_ref.shape[1]
    starts = [lax.bitwise_xor(here_ref[0], flip) * share for flip in range(GROUPS)]

    @pl.when(pl.program_id(0) == 0)
    def _():
        for flip, start in enumerate(starts):
            row = lax.broadcasted_iota(jnp.int32, (share, slots), 0) + start
            hit = row == target_ref[...]
            table_ref[pl.ds(flip * share, share), :] = jnp.where(hit, 1.0, 0.0).astype(jnp.bfloat16)

    total = jnp.dot(table_ref[...], part_ref[...], preferred_element_type=jnp.float32)
    for flip, (start, out_ref) in enumerate(zip(starts, out_refs)):
        head = head_ref[0, pl.ds(pl.multiple_of(start, share), share), :].astype(jnp.float32)
        block = total[flip * share : (flip + 1) * share, :] + head
        out_ref[...] = block.astype(out_ref.dtype)


def combine(here, target, head_grad, part, start, tile):
    slots = target.shape[1]
    width = part.shape[1]
    slab_rows = head_grad.shape[1]
    share = slab_rows // GROUPS
    return pl.pallas_call(
        combine_body,
        grid=(width // tile,),
        out_shape=[jax.ShapeDtypeStruct((share, width), jnp.float32)]
        + [jax.ShapeDtypeStruct((share, width), jnp.bfloat16)] * (GROUPS - 1),
        in_specs=[
            whole(pltpu.SMEM),
            pl.BlockSpec((1, slots), lambda i: (0, 0)),
            pl.BlockSpec((1, slab_rows, tile), lambda i: (0, 0, start // tile + i)),
            pl.BlockSpec((slots, tile), lambda i: (0, i)),
        ],
        out_specs=[pl.BlockSpec((share, tile), lambda i: (0, i))] * GROUPS,
        scratch_shapes=[pltpu.VMEM((slab_rows, slots), jnp.bfloat16)],
        compiler_params=pltpu.CompilerParams(vmem_limit_bytes=16 * MIB),
        cost_estimate=cost(2 * slab_rows * slots * width, (2 * slots + 5 * slab_rows) * width),
    )(here.reshape(1), target, head_grad, part)


def place_body(first, spots, share, here_ref, *refs):
    blocks, table_ref, sems = refs[first:-2], refs[-2], refs[-1]
    copies = []
    for at, (block, offset, flip, start) in enumerate(spots):
        row = pl.multiple_of(lax.bitwise_xor(here_ref[0], flip) * share, share)
        source = blocks[block]
        copies.append(
            pltpu.make_async_copy(
                source.at[pl.ds(offset, share), :],
                table_ref.at[pl.ds(row, share), pl.ds(start, source.shape[1])],
                sems.at[at],
            )
        )
    for copy in copies:
        copy.start()
    for copy in copies:
        copy.wait()


def place(table, here, blocks, spots, share, shape):
    before = [] if table is None else [table]
    return pl.pallas_call(
        functools.partial(place_body, len(before), spots, share),
        out_shape=jax.ShapeDtypeStruct(shape, jnp.bfloat16),
        in_specs=[whole(pltpu.SMEM)]
        + [whole(pl.ANY)] * len(before)
        + [whole(pltpu.VMEM)] * len(blocks),
        out_specs=whole(pl.ANY),
        scratch_shapes=[pltpu.SemaphoreType.DMA((len(spots),))],
        input_output_aliases={1: 0} if before else {},
        compiler_params=pltpu.CompilerParams(vmem_limit_bytes=8 * MIB),
        cost_estimate=cost(0, 4 * sum(block.size for block in blocks)),
    )(here.reshape(1), *before, *blocks)


def update(grad, master, moment_one, moment_two):
    first = beta_first * moment_one + (1.0 - beta_first) * grad
    second = beta_second * moment_two + (1.0 - beta_second) * grad * grad
    step_dir = (
        first / correct_first / (jnp.sqrt(second / correct_second) + epsilon)
        + weight_decay * master
    )
    return master - learn_rate * step_dir, first, second


def local(input_grad, token_slab, token_offset, head_grad, master, moment_one, moment_two):
    here, myself = lax.axis_index("dp"), lax.axis_index("vocab")
    tok_rows, width = input_grad.shape
    slab_rows = head_grad.shape[1]
    share = slab_rows // GROUPS
    slots = OWNERS * CAPACITY
    owners = token_slab[:, 0].reshape(OWNERS, tok_rows)
    offsets = token_offset[:, 0].reshape(OWNERS, tok_rows)

    order = jnp.arange(tok_rows, dtype=jnp.int32)
    earlier = (order[:, None] < order[None, :]).astype(jnp.bfloat16)

    own = lax.dynamic_slice_in_dim(token_slab, myself * tok_rows, tok_rows, 0)[:, 0]
    named = own[None, :] == jnp.arange(OWNERS, dtype=jnp.int32)[:, None]
    before = jnp.dot(named.astype(jnp.bfloat16), earlier, preferred_element_type=jnp.float32)
    own_rank = jnp.sum(jnp.where(named, before, 0.0), axis=0).astype(jnp.int32)
    slot_of = own * CAPACITY + own_rank
    slot_ids = jnp.arange(slots, dtype=jnp.int32)[:, None]

    dispatch = (slot_ids == slot_of[None, :]).astype(jnp.bfloat16)

    mine = owners == myself
    rank = jnp.dot(
        mine.astype(jnp.bfloat16), earlier, preferred_element_type=jnp.float32
    ).astype(jnp.int32)
    held = mine[:, None, :] & (
        rank[:, None, :] == jnp.arange(CAPACITY, dtype=jnp.int32)[None, :, None]
    )
    target = jnp.sum(jnp.where(held, offsets[:, None, :] + 1, 0), axis=2) - 1
    target = target.reshape(1, slots)

    unit = width // sum(UNITS)
    edges = [unit * sum(UNITS[:i]) for i in range(len(UNITS) + 1)]
    spans = [slice(low, high) for low, high in zip(edges, edges[1:])]
    states, rows, joined, fars, blocks, spots = [], [], [], [], [], []
    arrived, last = (), len(spans) - 1
    picked = [
        jnp.dot(dispatch, input_grad[:, span], preferred_element_type=jnp.float32).astype(jnp.bfloat16)
        for span in spans
    ]
    for number, span in enumerate(spans):
        outgoing = picked[number]
        earlier_work = (target, picked) if number == 1 else rows[: max(0, number - 1)]
        outgoing = after(outgoing, arrived, earlier_work, joined[: max(0, number - 1)])
        outgoing = after(outgoing, fars[: max(0, number - 2)])
        arrived = lax.all_to_all(outgoing, "vocab", split_axis=0, concat_axis=0, tiled=True)
        ready = after(arrived, rows)
        grad, *pieces = combine(here, target, head_grad, ready, span.start, TILE * unit)
        if number == last:
            pieces = after(pieces, fars[: number - 1])
        for flip, piece in enumerate(pieces, 1):
            grad = grad + swap_z(piece, flip).astype(jnp.float32)
        states.append(update(grad, master[:, span], moment_one[:, span], moment_two[:, span]))
        block = states[-1][0].astype(jnp.bfloat16)
        rows.append(block)
        if number < last:
            both = jnp.concatenate([block, swap_z(block, 3)], axis=0)
            joined.append(both)
            spots += [
                (len(blocks), 0, 0, span.start),
                (len(blocks), share, 3, span.start),
                (len(blocks) + 1, 0, 1, span.start),
                (len(blocks) + 1, share, 2, span.start),
            ]
            fars.append(swap_z(both, 1))
            blocks += [both, fars[-1]]
    shape = (slab_rows, width)
    blocks = after(blocks, rows)
    table = place(None, here, blocks, tuple(spots), share, shape)
    half = (span.stop - span.start) // 2
    blocks, spots = [], []
    for start, (one, two) in ((0, (1, 3)), (half, (3, 1))):
        part = block[:, start : start + half]
        both = jnp.concatenate([part, swap_z(part, one)], axis=0)
        spots += [
            (len(blocks), 0, 0, span.start + start),
            (len(blocks), share, one, span.start + start),
            (len(blocks) + 1, 0, two, span.start + start),
            (len(blocks) + 1, share, one ^ two, span.start + start),
        ]
        blocks += [both, swap_z(both, two)]
    table = place(table, here, blocks, tuple(spots), share, shape)
    return tuple(jnp.concatenate(parts, axis=1) for parts in zip(*states)) + (table,)


def solution(mesh):
    placed = (
        P(("dp", "vocab"), None),
        P("dp", None),
        P("dp", None),
        P("dp", "vocab", None),
        P(("vocab", "dp"), None),
        P(("vocab", "dp"), None),
        P(("vocab", "dp"), None),
    )
    return jax.shard_map(
        local,
        mesh=mesh,
        in_specs=placed,
        out_specs=(
            P(("vocab", "dp"), None),
            P(("vocab", "dp"), None),
            P(("vocab", "dp"), None),
            P("vocab", None),
        ),
        check_vma=False,
    )
```

```python
import functools

import jax
import jax.numpy as jnp
from jax import lax
from jax.experimental import pallas as pl
from jax.experimental.pallas import tpu as pltpu
from jax.sharding import PartitionSpec as P

beta_first = 0.9
beta_second = 0.95
learn_rate = 0.01
weight_decay = 0.1
epsilon = 1e-08
correct_first = 1.0 - 0.9**10
correct_second = 1.0 - 0.95**10

GROUPS = 4
OWNERS = 32
CAPACITY = 32
UNITS = (8, 10, 10, 8)
PLACES = (20, 0, 10, 28)
MIB = 1024 * 1024


def after(value, *others):
    return lax.optimization_barrier((value, others))[0]


def swap_z(block, flip):
    return lax.ppermute(block, "dp", [(i, i ^ flip) for i in range(GROUPS)])


def whole(memory_space):
    return pl.BlockSpec(memory_space=memory_space)


def cost(flops, moved):
    return pl.CostEstimate(flops=flops, bytes_accessed=moved, transcendentals=0)


def combine_body(here_ref, target_ref, head_ref, part_ref, own_ref, *refs):
    out_refs, table_ref = (own_ref,) + refs[:-1], refs[-1]
    share = own_ref.shape[0]
    slots = target_ref.shape[1]
    starts = [lax.bitwise_xor(here_ref[0], flip) * share for flip in range(GROUPS)]

    @pl.when(pl.program_id(0) == 0)
    def _():
        for flip, start in enumerate(starts):
            row = lax.broadcasted_iota(jnp.int32, (share, slots), 0) + start
            hit = row == target_ref[...]
            table_ref[pl.ds(flip * share, share), :] = jnp.where(hit, 1.0, 0.0).astype(jnp.bfloat16)

    total = jnp.dot(table_ref[...], part_ref[...], preferred_element_type=jnp.float32)
    for flip, (start, out_ref) in enumerate(zip(starts, out_refs)):
        head = head_ref[0, pl.ds(pl.multiple_of(start, share), share), :].astype(jnp.float32)
        block = total[flip * share : (flip + 1) * share, :] + head
        out_ref[...] = block.astype(out_ref.dtype)


def combine(here, target, head_grad, part, start):
    slots = target.shape[1]
    width = part.shape[1]
    slab_rows = head_grad.shape[1]
    share = slab_rows // GROUPS
    tile = width // 2
    return pl.pallas_call(
        combine_body,
        grid=(2,),
        out_shape=[jax.ShapeDtypeStruct((share, width), jnp.float32)]
        + [jax.ShapeDtypeStruct((share, width), jnp.bfloat16)] * (GROUPS - 1),
        in_specs=[
            whole(pltpu.SMEM),
            pl.BlockSpec((1, slots), lambda i: (0, 0)),
            pl.BlockSpec((1, slab_rows, tile), lambda i: (0, 0, start // tile + i)),
            pl.BlockSpec((slots, tile), lambda i: (0, i)),
        ],
        out_specs=[pl.BlockSpec((share, tile), lambda i: (0, i))] * GROUPS,
        scratch_shapes=[pltpu.VMEM((slab_rows, slots), jnp.bfloat16)],
        compiler_params=pltpu.CompilerParams(vmem_limit_bytes=16 * MIB),
        cost_estimate=cost(2 * slab_rows * slots * width, (2 * slots + 5 * slab_rows) * width),
    )(here.reshape(1), target, head_grad, part)


def place_body(first, spots, share, here_ref, *refs):
    blocks, table_ref, sems = refs[first:-2], refs[-2], refs[-1]
    copies = []
    for at, (block, offset, flip, start) in enumerate(spots):
        row = pl.multiple_of(lax.bitwise_xor(here_ref[0], flip) * share, share)
        source = blocks[block]
        copies.append(
            pltpu.make_async_copy(
                source.at[pl.ds(offset, share), :],
                table_ref.at[pl.ds(row, share), pl.ds(start, source.shape[1])],
                sems.at[at],
            )
        )
    for copy in copies:
        copy.start()
    for copy in copies:
        copy.wait()


def place(table, here, blocks, spots, share, shape):
    before = [] if table is None else [table]
    return pl.pallas_call(
        functools.partial(place_body, len(before), spots, share),
        out_shape=jax.ShapeDtypeStruct(shape, jnp.bfloat16),
        in_specs=[whole(pltpu.SMEM)]
        + [whole(pl.ANY)] * len(before)
        + [whole(pltpu.VMEM)] * len(blocks),
        out_specs=whole(pl.ANY),
        scratch_shapes=[pltpu.SemaphoreType.DMA((len(spots),))],
        input_output_aliases={1: 0} if before else {},
        compiler_params=pltpu.CompilerParams(vmem_limit_bytes=8 * MIB),
        cost_estimate=cost(0, 4 * sum(block.size for block in blocks)),
    )(here.reshape(1), *before, *blocks)


def update(grad, master, moment_one, moment_two):
    first = beta_first * moment_one + (1.0 - beta_first) * grad
    second = beta_second * moment_two + (1.0 - beta_second) * grad * grad
    step_dir = (
        first / correct_first / (jnp.sqrt(second / correct_second) + epsilon)
        + weight_decay * master
    )
    return master - learn_rate * step_dir, first, second


def local(input_grad, token_slab, token_offset, head_grad, master, moment_one, moment_two):
    here, myself = lax.axis_index("dp"), lax.axis_index("vocab")
    tok_rows, width = input_grad.shape
    slab_rows = head_grad.shape[1]
    share = slab_rows // GROUPS
    slots = OWNERS * CAPACITY
    owners = token_slab[:, 0].reshape(OWNERS, tok_rows)
    offsets = token_offset[:, 0].reshape(OWNERS, tok_rows)

    order = jnp.arange(tok_rows, dtype=jnp.int32)
    earlier = (order[:, None] < order[None, :]).astype(jnp.bfloat16)

    own = lax.dynamic_slice_in_dim(token_slab, myself * tok_rows, tok_rows, 0)[:, 0]
    named = own[None, :] == jnp.arange(OWNERS, dtype=jnp.int32)[:, None]
    before = jnp.dot(named.astype(jnp.bfloat16), earlier, preferred_element_type=jnp.float32)
    own_rank = jnp.sum(jnp.where(named, before, 0.0), axis=0).astype(jnp.int32)
    slot_of = own * CAPACITY + own_rank
    slot_ids = jnp.arange(slots, dtype=jnp.int32)[:, None]

    dispatch = (slot_ids == slot_of[None, :]).astype(jnp.bfloat16)

    mine = owners == myself
    rank = jnp.dot(
        mine.astype(jnp.bfloat16), earlier, preferred_element_type=jnp.float32
    ).astype(jnp.int32)
    held = mine[:, None, :] & (
        rank[:, None, :] == jnp.arange(CAPACITY, dtype=jnp.int32)[None, :, None]
    )
    target = jnp.sum(jnp.where(held, offsets[:, None, :] + 1, 0), axis=2) - 1
    target = target.reshape(1, slots)

    unit = width // sum(UNITS)
    spans = [slice(unit * at, unit * (at + size)) for at, size in zip(PLACES, UNITS)]
    states, rows, joined, fars, blocks, spots = [], [], [], [], [], []
    arrived, last = (), len(spans) - 1
    picked = [
        jnp.dot(dispatch, input_grad[:, span], preferred_element_type=jnp.float32).astype(jnp.bfloat16)
        for span in spans
    ]
    for number, span in enumerate(spans):
        outgoing = picked[number]
        earlier_work = (target, picked) if number == 1 else rows[: max(0, number - 1)]
        outgoing = after(outgoing, arrived, earlier_work, joined[: max(0, number - 1)])
        outgoing = after(outgoing, fars[: max(0, number - 2)])
        arrived = lax.all_to_all(outgoing, "vocab", split_axis=0, concat_axis=0, tiled=True)
        ready = after(arrived, rows)
        grad, *pieces = combine(here, target, head_grad, ready, span.start)
        if number == last:
            pieces = after(pieces, fars[: number - 1])
        for flip, piece in enumerate(pieces, 1):
            grad = grad + swap_z(piece, flip).astype(jnp.float32)
        states.append(update(grad, master[:, span], moment_one[:, span], moment_two[:, span]))
        block = states[-1][0].astype(jnp.bfloat16)
        rows.append(block)
        if number < last:
            both = jnp.concatenate([block, swap_z(block, 3)], axis=0)
            joined.append(both)
            spots += [
                (len(blocks), 0, 0, span.start),
                (len(blocks), share, 3, span.start),
                (len(blocks) + 1, 0, 1, span.start),
                (len(blocks) + 1, share, 2, span.start),
            ]
            fars.append(swap_z(both, 1))
            blocks += [both, fars[-1]]
    shape = (slab_rows, width)
    blocks = after(blocks, rows)
    table = place(None, here, blocks, tuple(spots), share, shape)
    half = (span.stop - span.start) // 2
    blocks, spots = [], []
    for start, (one, two) in ((0, (1, 3)), (half, (3, 1))):
        part = block[:, start : start + half]
        both = jnp.concatenate([part, swap_z(part, one)], axis=0)
        spots += [
            (len(blocks), 0, 0, span.start + start),
            (len(blocks), share, one, span.start + start),
            (len(blocks) + 1, 0, two, span.start + start),
            (len(blocks) + 1, share, one ^ two, span.start + start),
        ]
        blocks += [both, swap_z(both, two)]
    table = place(table, here, blocks, tuple(spots), share, shape)
    in_place = [states[number] for number in sorted(range(len(PLACES)), key=PLACES.__getitem__)]
    return tuple(jnp.concatenate(parts, axis=1) for parts in zip(*in_place)) + (table,)


def solution(mesh):
    placed = (
        P(("dp", "vocab"), None),
        P("dp", None),
        P("dp", None),
        P("dp", "vocab", None),
        P(("vocab", "dp"), None),
        P(("vocab", "dp"), None),
        P(("vocab", "dp"), None),
    )
    return jax.shard_map(
        local,
        mesh=mesh,
        in_specs=placed,
        out_specs=(
            P(("vocab", "dp"), None),
            P(("vocab", "dp"), None),
            P(("vocab", "dp"), None),
            P("vocab", None),
        ),
        check_vma=False,
    )
```

```python
import functools

import jax
import jax.numpy as jnp
from jax import lax
from jax.experimental import pallas as pl
from jax.experimental.pallas import tpu as pltpu
from jax.sharding import PartitionSpec as P

beta_first = 0.9
beta_second = 0.95
learn_rate = 0.01
weight_decay = 0.1
epsilon = 1e-08
correct_first = 1.0 - 0.9**10
correct_second = 1.0 - 0.95**10

GROUPS = 4
OWNERS = 32
CAPACITY = 32
UNITS = (8, 10, 10, 8)
PLACES = (20, 0, 10, 28)
MIB = 1024 * 1024


def after(value, *others):
    return lax.optimization_barrier((value, others))[0]


def swap_z(block, flip):
    return lax.ppermute(block, "dp", [(i, i ^ flip) for i in range(GROUPS)])


def whole(memory_space):
    return pl.BlockSpec(memory_space=memory_space)


def cost(flops, moved):
    return pl.CostEstimate(flops=flops, bytes_accessed=moved, transcendentals=0)


def combine_body(here_ref, target_ref, head_ref, part_ref, own_ref, *refs):
    out_refs, table_ref = (own_ref,) + refs[:-1], refs[-1]
    share = own_ref.shape[0]
    slots = target_ref.shape[1]
    starts = [lax.bitwise_xor(here_ref[0], flip) * share for flip in range(GROUPS)]

    @pl.when(pl.program_id(0) == 0)
    def _():
        for flip, start in enumerate(starts):
            row = lax.broadcasted_iota(jnp.int32, (share, slots), 0) + start
            hit = row == target_ref[...]
            table_ref[pl.ds(flip * share, share), :] = jnp.where(hit, 1.0, 0.0).astype(jnp.bfloat16)

    total = jnp.dot(table_ref[...], part_ref[...], preferred_element_type=jnp.float32)
    for flip, (start, out_ref) in enumerate(zip(starts, out_refs)):
        head = head_ref[0, pl.ds(pl.multiple_of(start, share), share), :].astype(jnp.float32)
        block = total[flip * share : (flip + 1) * share, :] + head
        out_ref[...] = block.astype(out_ref.dtype)


def combine(here, target, head_grad, part, start):
    slots = target.shape[1]
    width = part.shape[1]
    slab_rows = head_grad.shape[1]
    share = slab_rows // GROUPS
    tile = width // 2
    return pl.pallas_call(
        combine_body,
        grid=(2,),
        out_shape=[jax.ShapeDtypeStruct((share, width), jnp.float32)]
        + [jax.ShapeDtypeStruct((share, width), jnp.bfloat16)] * (GROUPS - 1),
        in_specs=[
            whole(pltpu.SMEM),
            pl.BlockSpec((1, slots), lambda i: (0, 0)),
            pl.BlockSpec((1, slab_rows, tile), lambda i: (0, 0, start // tile + i)),
            pl.BlockSpec((slots, tile), lambda i: (0, i)),
        ],
        out_specs=[pl.BlockSpec((share, tile), lambda i: (0, i))] * GROUPS,
        scratch_shapes=[pltpu.VMEM((slab_rows, slots), jnp.bfloat16)],
        compiler_params=pltpu.CompilerParams(vmem_limit_bytes=16 * MIB),
        cost_estimate=cost(2 * slab_rows * slots * width, (2 * slots + 5 * slab_rows) * width),
    )(here.reshape(1), target, head_grad, part)


def place_body(first, spots, share, here_ref, *refs):
    blocks, table_ref, sems = refs[first:-2], refs[-2], refs[-1]
    copies = []
    for at, (block, offset, flip, start) in enumerate(spots):
        row = pl.multiple_of(lax.bitwise_xor(here_ref[0], flip) * share, share)
        source = blocks[block]
        copies.append(
            pltpu.make_async_copy(
                source.at[pl.ds(offset, share), :],
                table_ref.at[pl.ds(row, share), pl.ds(start, source.shape[1])],
                sems.at[at],
            )
        )
    for copy in copies:
        copy.start()
    for copy in copies:
        copy.wait()


def place(table, here, blocks, spots, share, shape):
    before = [] if table is None else [table]
    return pl.pallas_call(
        functools.partial(place_body, len(before), spots, share),
        out_shape=jax.ShapeDtypeStruct(shape, jnp.bfloat16),
        in_specs=[whole(pltpu.SMEM)]
        + [whole(pl.ANY)] * len(before)
        + [whole(pltpu.VMEM)] * len(blocks),
        out_specs=whole(pl.ANY),
        scratch_shapes=[pltpu.SemaphoreType.DMA((len(spots),))],
        input_output_aliases={1: 0} if before else {},
        compiler_params=pltpu.CompilerParams(vmem_limit_bytes=8 * MIB),
        cost_estimate=cost(0, 4 * sum(block.size for block in blocks)),
    )(here.reshape(1), *before, *blocks)


def update(grad, master, moment_one, moment_two):
    first = beta_first * moment_one + (1.0 - beta_first) * grad
    second = beta_second * moment_two + (1.0 - beta_second) * grad * grad
    step_dir = (
        first / correct_first / (jnp.sqrt(second / correct_second) + epsilon)
        + weight_decay * master
    )
    return master - learn_rate * step_dir, first, second


def local(input_grad, token_slab, token_offset, head_grad, master, moment_one, moment_two):
    here, myself = lax.axis_index("dp"), lax.axis_index("vocab")
    tok_rows, width = input_grad.shape
    slab_rows = head_grad.shape[1]
    share = slab_rows // GROUPS
    slots = OWNERS * CAPACITY
    owners = token_slab[:, 0].reshape(OWNERS, tok_rows)
    offsets = token_offset[:, 0].reshape(OWNERS, tok_rows)

    order = jnp.arange(tok_rows, dtype=jnp.int32)
    earlier = (order[:, None] < order[None, :]).astype(jnp.bfloat16)

    own = lax.dynamic_slice_in_dim(token_slab, myself * tok_rows, tok_rows, 0)[:, 0]
    named = own[None, :] == jnp.arange(OWNERS, dtype=jnp.int32)[:, None]
    before = jnp.dot(named.astype(jnp.bfloat16), earlier, preferred_element_type=jnp.float32)
    own_rank = jnp.sum(jnp.where(named, before, 0.0), axis=0).astype(jnp.int32)
    slot_of = own * CAPACITY + own_rank
    slot_ids = jnp.arange(slots, dtype=jnp.int32)[:, None]

    dispatch = (slot_ids == slot_of[None, :]).astype(jnp.bfloat16)

    mine = owners == myself
    rank = jnp.dot(
        mine.astype(jnp.bfloat16), earlier, preferred_element_type=jnp.float32
    ).astype(jnp.int32)
    held = mine[:, None, :] & (
        rank[:, None, :] == jnp.arange(CAPACITY, dtype=jnp.int32)[None, :, None]
    )
    target = jnp.sum(jnp.where(held, offsets[:, None, :] + 1, 0), axis=2) - 1
    target = target.reshape(1, slots)

    unit = width // sum(UNITS)
    spans = [slice(unit * at, unit * (at + size)) for at, size in zip(PLACES, UNITS)]
    states, rows, joined, fars, blocks, spots = [], [], [], [], [], []
    arrived, last = (), len(spans) - 1
    picked = [
        jnp.dot(dispatch, input_grad[:, span], preferred_element_type=jnp.float32).astype(jnp.bfloat16)
        for span in spans
    ]
    for number, span in enumerate(spans):
        outgoing = picked[number]
        earlier_work = (target, picked) if number == 1 else rows[: max(0, number - 1)]
        outgoing = after(outgoing, arrived, earlier_work, joined[: max(0, number - 1)])
        outgoing = after(outgoing, fars[: max(0, number - 2)])
        arrived = lax.all_to_all(outgoing, "vocab", split_axis=0, concat_axis=0, tiled=True)
        ready = after(arrived, rows)
        grad, *pieces = combine(here, target, head_grad, ready, span.start)
        if number == last:
            pieces = after(pieces, fars[: number - 1])
        for flip, piece in enumerate(pieces, 1):
            grad = grad + swap_z(piece, flip).astype(jnp.float32)
        states.append(update(grad, master[:, span], moment_one[:, span], moment_two[:, span]))
        block = states[-1][0].astype(jnp.bfloat16)
        rows.append(block)
        if number < last:
            cuts = [(0, (3, 1))] if number < last - 1 else [(0, (1, 3)), (block.shape[1] // 2, (3, 1))]
            size = block.shape[1] // len(cuts)
            for start, (one, two) in cuts:
                part = block[:, start : start + size]
                both = jnp.concatenate([part, swap_z(part, one)], axis=0)
                joined.append(both)
                fars.append(swap_z(both, two))
                spots += [
                    (len(blocks), 0, 0, span.start + start),
                    (len(blocks), share, one, span.start + start),
                    (len(blocks) + 1, 0, two, span.start + start),
                    (len(blocks) + 1, share, one ^ two, span.start + start),
                ]
                blocks += [both, fars[-1]]
    shape = (slab_rows, width)
    blocks = after(blocks, rows)
    table = place(None, here, blocks, tuple(spots), share, shape)
    half = (span.stop - span.start) // 2
    blocks, spots = [], []
    for start, (one, two) in ((0, (1, 3)), (half, (3, 1))):
        part = block[:, start : start + half]
        both = jnp.concatenate([part, swap_z(part, one)], axis=0)
        spots += [
            (len(blocks), 0, 0, span.start + start),
            (len(blocks), share, one, span.start + start),
            (len(blocks) + 1, 0, two, span.start + start),
            (len(blocks) + 1, share, one ^ two, span.start + start),
        ]
        blocks += [both, swap_z(both, two)]
    table = place(table, here, blocks, tuple(spots), share, shape)
    in_place = [states[number] for number in sorted(range(len(PLACES)), key=PLACES.__getitem__)]
    return tuple(jnp.concatenate(parts, axis=1) for parts in zip(*in_place)) + (table,)


def solution(mesh):
    placed = (
        P(("dp", "vocab"), None),
        P("dp", None),
        P("dp", None),
        P("dp", "vocab", None),
        P(("vocab", "dp"), None),
        P(("vocab", "dp"), None),
        P(("vocab", "dp"), None),
    )
    return jax.shard_map(
        local,
        mesh=mesh,
        in_specs=placed,
        out_specs=(
            P(("vocab", "dp"), None),
            P(("vocab", "dp"), None),
            P(("vocab", "dp"), None),
            P("vocab", None),
        ),
        check_vma=False,
    )
```
